128 devices in a mesh: dp: 2 (over y_hi), seq: 8 (over y_lo, x), tensor: 8 (over z, core).
Axes of the slice: x: 4, y: 4 (y_hi: 2, y_lo: 2; y = y_hi * 2 + y_lo), z: 4, core: 2. Of those that a mesh axis runs over, the one named last changes fastest.
Arguments:
- tokens: bfloat16 [16384, 2048], P(('dp', 'seq')), parts along dimension 0, may hold values from -6 to 6
- doc_ids: int32 [16384], P('dp'), parts along dimension 0, may hold values from 0 to 3, never falling along the last dimension, each value on 1 to 4096 neighbouring positions
- mlp_gain: bfloat16 [2048], replicated, may hold values from 0.099609375 to 1.8984375
- gate_weight: bfloat16 [2048, 8192], P(None, 'tensor'), may hold values from -0.125 to 0.125
- up_weight: bfloat16 [2048, 8192], P(None, 'tensor'), may hold values from -0.125 to 0.125
- down_weight: bfloat16 [8192, 2048], P('tensor'), may hold values from -0.0625 to 0.0625
- attn_gain: bfloat16 [2048], replicated, may hold values from 0.099609375 to 1.8984375
- query_weight: bfloat16 [2048, 2048], P(None, 'tensor'), may hold values from -8 to 8
- key_weight: bfloat16 [2048, 2048], P(None, 'tensor'), may hold values from -1 to 1
- value_weight: bfloat16 [2048, 2048], P(None, 'tensor'), may hold values from -0.125 to 0.125
- out_weight: bfloat16 [2048, 2048], P('tensor'), may hold values from -0.125 to 0.125
Outputs:
- layer_out: bfloat16 [16384, 2048], P(('dp', 'seq', 'tensor')), parts along dimension 0
The draws below stay inside these ranges and needn't reach their ends.
There are 2 independent parts, one for each index of `dp`. The reference program is written for one: setup_inputs(seed, part) draws one part's arguments, and reference() takes and returns one part's arrays. A program takes and returns all parts, laid end to end along the dimension named above; an argument that names none is the same for every part. Nothing has to cross between parts.
Inputs may be any that keep to these rules, and one draw needn't show every extreme that they name: doc_ids never falls along the positions; each document covers 1 to 4096 positions, one of them exactly 4096.
All inputs are finite; a program needn't handle non-finite values.
Results may differ from the reference program's by a relative error of at most 0.01325.
Values may be sent and summed in bfloat16 or wider, within the bound.
A program may use at most 128 MiB of HBM per device.

```python
import math
import jax
import jax.numpy as jnp
import numpy as np
from jax import lax

D = 2048
FF = 8192
HEADS = 16
HEAD_DIM = 128
DOCS = 4
ROWS_DEV = 1024
LENGTH = 8192
N_SEQ = 8
N_TENSOR = 8


def shared_columns(key):
    return jax.random.normal(key, (D, HEADS * HEAD_DIM), jnp.float32)


def draw_key_weight(key, part):
    shared = shared_columns(key)
    key = jax.random.fold_in(key, 11)
    own_part = jax.random.normal(key, (D, HEADS * HEAD_DIM), jnp.float32)
    return ((0.6 * shared + 0.8 * own_part) * D ** (-0.5)).astype(jnp.bfloat16)


def draw_query_weight(key, part):
    key = jax.random.fold_in(key, 7)
    own_part = jax.random.normal(key, (D, HEADS * HEAD_DIM), jnp.float32)
    mixed = own_part
    return jnp.clip(mixed * D ** (-0.5), -8.0, 8.0).astype(jnp.bfloat16)


def block_levels(key, dims, pieces, low, top_value):
    loudness, own = 1.0, jax.random.fold_in(key, 6)
    for dim, blocks in pieces:
        steps = jnp.exp(jax.random.uniform(jax.random.fold_in(own, dim), (blocks,), jnp.float32, low / len(pieces), top_value / len(pieces)))
        loudness = loudness * jnp.repeat(steps, dims[dim] // blocks).reshape([-1 if axis == dim else 1 for axis in range(len(dims))])
    return loudness


def split_up(count, total, bound, skew):
    loads = [(1 << 20) // math.isqrt(standing ** skew) + 1 for standing in range(2, count + 1)]
    surplus, counts = total - bound - (count - 1), [1] * (count - 1)
    while surplus > 0:
        free = [i for i in range(count - 1) if counts[i] < bound]
        pool, budget = sum([loads[i] for i in free]), surplus
        for i in free:
            extra = min(bound - counts[i], max(1, budget * loads[i] // pool), surplus)
            counts[i] = counts[i] + extra
            surplus = surplus - extra
    return np.array([bound] + counts)


def ragged(key, number_of, total, limit, slope):
    if number_of == 2:
        one = jax.random.randint(key, (), max(1, total - limit), min(limit, total - 1) + 1)
        return jnp.stack([one, total - one])
    lengths = jnp.asarray(split_up(number_of, total, limit, slope), jnp.int32)
    twos = (number_of - 1) // 2
    giver, receiver = lengths[1:1 + 2 * twos:2], lengths[2:2 + 2 * twos:2]
    room = jnp.minimum(giver - 1, limit - receiver)
    moved = jax.random.randint(jax.random.fold_in(key, 1), (twos,), 0, 1 << 20) % (room + 1)
    lengths = lengths.at[1:1 + 2 * twos:2].set(giver - moved).at[2:2 + 2 * twos:2].set(receiver + moved)
    return lengths[jax.random.permutation(jax.random.fold_in(key, 2), number_of)]


def scatter_about(key, extent, width, limit, pieces=(), kind=jnp.bfloat16):
    array = jax.random.normal(key, extent, jnp.float32) * width
    if len(pieces) > 0:
        array = block_levels(key, extent, pieces, -0.22, 0.18) * array
    return jnp.clip(array, min=-limit, max=limit).astype(kind)


def setup_inputs(seed: int = 0, part: int = 0) -> dict:
    key_of = jax.random.split(jax.random.key(seed), 12)
    part_splits = jax.random.split(jax.random.fold_in(key_of[11], part), 12)
    tokens = scatter_about(part_splits[0], (LENGTH, D), 1.0, 6.0, ((0, 8),))
    doc_ids = jnp.searchsorted(jnp.cumsum(ragged(part_splits[1], DOCS, LENGTH, LENGTH // 2, 2)), jnp.arange(LENGTH), side="right").astype(jnp.int32)
    mlp_gain = jnp.clip(1.0 + 0.18 * jax.random.normal(key_of[2], (D,), jnp.float32), 0.099609375, 1.8984375).astype(jnp.bfloat16)
    gate_weight = scatter_about(key_of[3], (D, FF), D ** -0.5, 0.125, ((1, 8),))
    up_weight = scatter_about(key_of[4], (D, FF), D ** -0.5, 0.125, ((1, 8),))
    down_weight = scatter_about(key_of[5], (FF, D), FF ** -0.5, 0.0625, ((0, 8),))
    attn_gain = jnp.clip(1.0 + 0.18 * jax.random.normal(key_of[6], (D,), jnp.float32), 0.099609375, 1.8984375).astype(jnp.bfloat16)
    query_weight = draw_query_weight(jax.random.fold_in(key_of[11], 71), part)
    key_weight = draw_key_weight(jax.random.fold_in(key_of[11], 71), part)
    value_weight = scatter_about(key_of[9], (D, HEADS * HEAD_DIM), D ** -0.5, 0.125, ((1, 8),))
    out_weight = scatter_about(key_of[10], (HEADS * HEAD_DIM, D), (HEADS * HEAD_DIM) ** -0.5, 0.125, ((0, 8),))
    return dict(tokens=tokens, doc_ids=doc_ids, mlp_gain=mlp_gain, gate_weight=gate_weight, up_weight=up_weight, down_weight=down_weight, attn_gain=attn_gain, query_weight=query_weight, key_weight=key_weight, value_weight=value_weight, out_weight=out_weight)


EPSILON = 1e-05
ROPE_BASE = 500000.0
NEGATIVE = -1e+30

def rms_scale(values, gain):
    mean_square = lax.optimization_barrier(jnp.mean(values * values, axis=-1, keepdims=True))
    return values * lax.rsqrt(mean_square + EPSILON) * gain.astype(jnp.float32)

def row_positions(seq_group, local_rows, rows_dev, groups, splits):
    slice_rows = rows_dev // (groups * splits)
    half_rows = rows_dev // (2 * groups)
    tensor_part = local_rows // (groups * slice_rows)
    source_group = local_rows // slice_rows % groups
    within = local_rows % slice_rows
    offset = tensor_part * slice_rows + within
    which_block = jnp.where(offset < half_rows, seq_group, 2 * groups - 1 - seq_group)
    return (source_group * rows_dev + which_block * half_rows + offset % half_rows).astype(jnp.int32)

def rotate(values, positions, head_dim):
    row_count = values.shape[0]
    shaped = values.reshape(row_count, -1, head_dim)
    half_dim = head_dim // 2
    frequency = ROPE_BASE ** (-(jnp.arange(half_dim, dtype=jnp.float32) / half_dim))
    angles = positions.astype(jnp.float32)[:, None] * frequency[None, :]
    cosine = jnp.cos(angles)[:, None, :]
    sine_part = jnp.sin(angles)[:, None, :]
    front_half = shaped[..., :half_dim]
    back_half = shaped[..., half_dim:]
    turned = jnp.concatenate([front_half * cosine - back_half * sine_part, back_half * cosine + front_half * sine_part], axis=-1)
    return turned.reshape(row_count, -1)

def reference(tokens, doc_ids, mlp_gain, gate_weight, up_weight, down_weight, attn_gain, query_weight, key_weight, value_weight, out_weight):
    length = tokens.shape[0]
    stream_in = tokens.astype(jnp.float32)
    mlp_in = rms_scale(stream_in, mlp_gain).astype(jnp.bfloat16)
    gate = jnp.dot(mlp_in, gate_weight, preferred_element_type=jnp.float32)
    up_part = jnp.dot(mlp_in, up_weight, preferred_element_type=jnp.float32)
    hidden = (jax.nn.silu(gate) * up_part).astype(jnp.bfloat16)
    stream = (stream_in + jnp.dot(hidden, down_weight, preferred_element_type=jnp.float32)).astype(jnp.bfloat16)
    attn_in = rms_scale(stream.astype(jnp.float32), attn_gain).astype(jnp.bfloat16)
    positions = jnp.arange(length, dtype=jnp.int32)
    queries = rotate(jnp.dot(attn_in, query_weight, preferred_element_type=jnp.float32), positions, HEAD_DIM).astype(jnp.bfloat16)
    key_rows = rotate(jnp.dot(attn_in, key_weight, preferred_element_type=jnp.float32), positions, HEAD_DIM).astype(jnp.bfloat16)
    value_rows = jnp.dot(attn_in, value_weight, preferred_element_type=jnp.float32).astype(jnp.bfloat16)
    score_scale = HEAD_DIM ** (-0.5)

    def one_head(head_index):
        head_start = (head_index * HEAD_DIM).astype(jnp.int32)
        head_keys = lax.dynamic_slice_in_dim(key_rows, head_start, HEAD_DIM, 1)
        head_values = lax.dynamic_slice_in_dim(value_rows, head_start, HEAD_DIM, 1)

        def one_block(block_index):
            first_row = (block_index * ROWS_DEV).astype(jnp.int32)
            head_queries = lax.dynamic_slice(queries, (first_row, head_start), (ROWS_DEV, HEAD_DIM))
            query_pos = first_row + jnp.arange(ROWS_DEV, dtype=jnp.int32)
            query_docs = lax.dynamic_slice_in_dim(doc_ids, first_row, ROWS_DEV, 0)
            allowed = (positions[None, :] <= query_pos[:, None]) & (doc_ids[None, :] == query_docs[:, None])
            scores = jnp.dot(head_queries, head_keys.T, preferred_element_type=jnp.float32) * score_scale
            scores = jnp.where(allowed, scores, NEGATIVE)
            highest = lax.optimization_barrier(jnp.max(scores, axis=1, keepdims=True))
            weights = jnp.where(allowed, jnp.exp(scores - highest), 0.0)
            totals = lax.optimization_barrier(jnp.sum(weights, axis=1, keepdims=True))
            mixed = jnp.dot(weights.astype(jnp.bfloat16), head_values, preferred_element_type=jnp.float32)
            return (mixed / totals).astype(jnp.bfloat16)
        return lax.map(one_block, jnp.arange(N_SEQ, dtype=jnp.int32))
    context = lax.map(one_head, jnp.arange(HEADS, dtype=jnp.int32))
    context = jnp.transpose(context, (1, 2, 0, 3)).reshape(length, HEADS * HEAD_DIM)
    merged = (stream.astype(jnp.float32) + jnp.dot(context, out_weight, preferred_element_type=jnp.float32)).astype(jnp.bfloat16)
    out_rows = jnp.arange(length, dtype=jnp.int32)
    order = row_positions(out_rows // ROWS_DEV, out_rows % ROWS_DEV, ROWS_DEV, N_SEQ, N_TENSOR)
    return merged[order]
```

```python
import functools

import jax
import jax.numpy as jnp
import numpy as np
from jax import lax
from jax.experimental import pallas as pl
from jax.experimental.pallas import tpu as pltpu
from jax.sharding import PartitionSpec as P

HEAD_DIM = 128
EPSILON = 1e-05
ROPE_BASE = 500000.0
NEGATIVE = -1e30
MESH = pl.DeviceIdType.MESH
F32 = jnp.float32
BF16 = jnp.bfloat16
VMEM_LIMIT = 60 * 1024 * 1024


def place():
    s = lax.axis_index("seq")
    c = lax.axis_index("tensor")
    return s, c, s // 4, s % 4, c // 2, c % 2


def remote(src, dst, send_sem, recv_sem, seq, tensor):
    return pltpu.make_async_remote_copy(
        src_ref=src,
        dst_ref=dst,
        send_sem=send_sem,
        recv_sem=recv_sem,
        device_id={"dp": lax.axis_index("dp"), "seq": seq, "tensor": tensor},
        device_id_type=MESH,
    )


def arrived(dst, recv_sem):
    pltpu.make_async_copy(dst, dst, recv_sem).wait()


def greet(partners):
    barrier = pltpu.get_barrier_semaphore()
    for seq, tensor in partners:
        pl.semaphore_signal(
            barrier,
            inc=1,
            device_id={"dp": lax.axis_index("dp"), "seq": seq, "tensor": tensor},
            device_id_type=MESH,
        )
    pl.semaphore_wait(barrier, len(partners))


def normalized(values, gain):
    mean_square = jnp.mean(values * values, axis=-1, keepdims=True)
    return (values * lax.rsqrt(mean_square + EPSILON) * gain).astype(BF16)


class RingSum:
    def __init__(self, send, recv, send_sem, recv_sem, s, z, k):
        self.send, self.recv = send, recv
        self.send_sem, self.recv_sem = send_sem, recv_sem
        self.s, self.z = s, z
        self.up = (z + 1) % 4
        self.down = (z + 3) % 4
        self.far = (z + 2) % 4
        self.up_c = self.up * 2 + k
        self.down_c = self.down * 2 + k

    def copies(self, ch, phase):
        part = pl.ds(0, 2) if phase == 0 else pl.ds(2, 1)
        made = []
        for d, target in ((0, self.up_c), (1, self.down_c)):
            made.append(
                remote(
                    self.send.at[ch, d, part],
                    self.recv.at[ch, d, part],
                    self.send_sem.at[ch, d, phase],
                    self.recv_sem.at[ch, d, phase],
                    self.s,
                    target,
                )
            )
        return made

    def first(self, ch, value):
        self.send[ch, 0, 0] = value(self.far, 0).astype(BF16)
        self.send[ch, 0, 1] = value(self.up, 1).astype(BF16)
        self.send[ch, 1, 0] = value(self.far, 1).astype(BF16)
        self.send[ch, 1, 1] = value(self.down, 0).astype(BF16)
        for copy in self.copies(ch, 0):
            copy.start()

    def second(self, ch, value):
        for copy in self.copies(ch, 0):
            copy.wait_recv()
        self.send[ch, 0, 2] = (value(self.up, 0) + self.recv[ch, 0, 0].astype(F32)).astype(BF16)
        self.send[ch, 1, 2] = (value(self.down, 1) + self.recv[ch, 1, 0].astype(F32)).astype(BF16)
        for copy in self.copies(ch, 1):
            copy.start()

    def third(self, ch, value):
        for copy in self.copies(ch, 1):
            copy.wait_recv()
        one = (
            value(self.z, 0)
            + self.recv[ch, 0, 2].astype(F32)
            + self.recv[ch, 1, 1].astype(F32)
        )
        two = (
            value(self.z, 1)
            + self.recv[ch, 0, 1].astype(F32)
            + self.recv[ch, 1, 2].astype(F32)
        )
        return one, two

    def finish(self, ch):
        for phase in range(2):
            for copy in self.copies(ch, phase):
                copy.wait_send()


def ff_kernel(
    tok_hbm, gain_ref, wg_hbm, wu_hbm, wd_hbm, q_hbm, k_hbm, v_hbm, o_hbm,
    stream_ref, sq_hbm, sk_hbm, sv_hbm, so_hbm,
    tok, wg, wu, wd, xn, hid, mine, csend, crecv, zsend, zrecv, sstage,
    tok_sem, gu_sem, wd_sem, wsem_s, wsem_r, csem_s, csem_r, zsem_s, zsem_r, ssem_s, ssem_r, own_sem,
):
    s, c, y, x, z, k = place()
    sib = c + 1 - 2 * k
    ff = wg.shape[1]
    width = tok.shape[1]
    gu_tiles = 4
    gu_cols = ff // gu_tiles

    def pair_of(ch):
        return (s // 2 + 1 + ch) % 4

    def tok_copies(ch):
        a = pair_of(ch) * 2
        low = pl.ds(pl.multiple_of(a * 64, 128), 128)
        high = pl.ds(pl.multiple_of((14 - a) * 64, 128), 128)
        return [
            pltpu.make_async_copy(tok_hbm.at[low], tok.at[low], tok_sem.at[ch, 0]),
            pltpu.make_async_copy(tok_hbm.at[high], tok.at[high], tok_sem.at[ch, 1]),
        ]

    def gu_copies(n):
        cols = pl.ds(n * gu_cols, gu_cols)
        return [
            pltpu.make_async_copy(wg_hbm.at[:, cols], wg.at[:, cols], gu_sem.at[n, 0]),
            pltpu.make_async_copy(wu_hbm.at[:, cols], wu.at[:, cols], gu_sem.at[n, 1]),
        ]

    wd_copy = pltpu.make_async_copy(wd_hbm, wd, wd_sem.at[0])
    for copy in tok_copies(0):
        copy.start()
    for n in range(gu_tiles):
        for copy in gu_copies(n):
            copy.start()
    wd_copy.start()
    for ch in range(1, 4):
        for copy in tok_copies(ch):
            copy.start()

    ring = RingSum(zsend, zrecv, zsem_s, zsem_r, s, z, k)
    partners = [(s, sib), (s, ring.up_c), (s, ring.down_c)]
    partners += [((s + d) % 8, c) for d in range(1, 8)]
    greet(partners)

    weight_sends = [
        remote(src, dst, wsem_s.at[i], wsem_r.at[i], s, sib)
        for i, (src, dst) in enumerate(
            ((q_hbm, sq_hbm), (k_hbm, sk_hbm), (v_hbm, sv_hbm), (o_hbm, so_hbm))
        )
    ]

    def token_rows(ch):
        a = pair_of(ch) * 2
        low = tok[pl.ds(pl.multiple_of(a * 64, 128), 128), :]
        high = tok[pl.ds(pl.multiple_of((14 - a) * 64, 128), 128), :]
        return low, high

    def gate_tile(cols):
        gate = jnp.dot(xn[...], wg[:, cols], preferred_element_type=F32)
        up = jnp.dot(xn[...], wu[:, cols], preferred_element_type=F32)
        hid[:, cols] = (gate / (1.0 + jnp.exp(-gate)) * up).astype(BF16)

    def hidden(ch):
        for copy in tok_copies(ch):
            copy.wait()
        low, high = token_rows(ch)
        gain = gain_ref[...].astype(F32)
        xn[0:128, :] = normalized(low.astype(F32), gain)
        xn[128:256, :] = normalized(high.astype(F32), gain)
        if ch == 0:
            for n in range(gu_tiles):
                for copy in gu_copies(n):
                    copy.wait()
                gate_tile(pl.ds(n * gu_cols, gu_cols))
        else:

            @pl.loop(0, gu_tiles)
            def _(n):
                gate_tile(pl.ds(pl.multiple_of(n * gu_cols, gu_cols), gu_cols))

    def core_copy(ch):
        return remote(csend.at[ch], crecv.at[ch], csem_s.at[ch], csem_r.at[ch], s, sib)

    def down(ch):
        if ch == 0:
            wd_copy.wait()
        cols_n = 256

        @pl.loop(0, width // cols_n)
        def _(n):
            cols = pl.ds(pl.multiple_of(n * cols_n, cols_n), cols_n)
            part = jnp.dot(hid[...], wd[:, cols], preferred_element_type=F32)
            part = part.reshape(4, 2, 2, 16, cols_n)
            even, odd = part[:, :, 0], part[:, :, 1]
            mine[ch, :, :, :, cols] = jnp.where(k == 0, even, odd)
            csend[ch, :, :, :, cols] = jnp.where(k == 0, odd, even).astype(BF16)

        core_copy(ch).start()

    def piece(ch):
        def value(zd, t):
            block = jnp.where(zd < 2, t, 3 - t)
            return mine[ch, block, zd % 2] + crecv[ch, block, zd % 2].astype(F32)

        return value

    def first(ch):
        core_copy(ch).wait_recv()
        ring.first(ch, piece(ch))

    def second(ch):
        ring.second(ch, piece(ch))

    def seq_copy(ch, t, target):
        return remote(
            sstage.at[ch, t], stream_ref.at[s], ssem_s.at[ch, t], ssem_r.at[s], target, c
        )

    def third(ch):
        totals = ring.third(ch, piece(ch))
        a = pair_of(ch) * 2
        for t in range(2):
            block = jnp.where(z < 2, a + t, 15 - a - t)
            start = pl.multiple_of(block * 64 + (2 * (z % 2) + k) * 16, 16)
            rows = tok[pl.ds(start, 16), :].astype(F32)
            sstage[ch, t] = (totals[t] + rows).astype(BF16)
            if ch < 3:
                seq_copy(ch, t, a + t).start()
            else:

                @pl.when(s == a + t)
                def _():
                    pltpu.make_async_copy(sstage.at[ch, t], stream_ref.at[s], own_sem.at[0]).start()

                @pl.when(s != a + t)
                def _():
                    seq_copy(ch, t, a + t).start()

    hidden(0)
    down(0)
    for copy in weight_sends:
        copy.start()
    hidden(1)
    first(0)
    down(1)
    hidden(2)
    first(1)
    second(0)
    down(2)
    hidden(3)
    first(2)
    second(1)
    third(0)
    down(3)
    second(2)
    third(1)
    first(3)
    third(2)
    second(3)
    third(3)

    for ch in range(4):
        core_copy(ch).wait_send()
        ring.finish(ch)
        a = pair_of(ch) * 2
        for t in range(2):
            if ch < 3:
                seq_copy(ch, t, a + t).wait_send()
            else:

                @pl.when(s == a + t)
                def _():
                    pltpu.make_async_copy(sstage.at[ch, t], stream_ref.at[s], own_sem.at[0]).wait()

                @pl.when(s != a + t)
                def _():
                    seq_copy(ch, t, a + t).wait_send()

    for d in range(1, 8):
        g = (s + d) % 8
        arrived(stream_ref.at[g], ssem_r.at[g])
    for copy in weight_sends:
        copy.wait()


def rope_table(groups, base_rows):
    half = HEAD_DIM // 2
    frequency = ROPE_BASE ** (-(np.arange(half, dtype=np.float64) / half))
    angles = np.arange(groups * base_rows, dtype=np.float64)[:, None] * frequency[None, :]
    cosine, sine = np.cos(angles), np.sin(angles)
    table = np.concatenate([cosine, cosine, -sine, sine], axis=1).astype(np.float32)
    return table.reshape(groups, 16, 2, 2, 16, 4 * half)


def qkv_kernel(
    stream_ref, gain_ref, q_hbm, k_hbm, v_hbm, sq_hbm, sk_hbm, sv_hbm, table_hbm,
    q_out, kv_out,
    xg, w, tab, qst, kvst,
    w_sem, tab_sem,
    own_s, own_r, relay_s, relay_r, q_s, q_r, kv_s, kv_r, yf_s, yf_r, f1_s, f1_r, f2_s, f2_r,
):
    s, c, y, x, z, k = place()
    sib = c + 1 - 2 * k
    up_c = ((z + 1) % 4) * 2 + k
    down_c = ((z + 3) % 4) * 2 + k
    up, down, far = (z + 1) % 4, (z + 3) % 4, (z + 2) % 4
    other_s = (1 - y) * 4 + x

    weight_copies = [
        pltpu.make_async_copy(src, w.at[i], w_sem.at[i])
        for i, src in enumerate((q_hbm, k_hbm, v_hbm, sq_hbm, sk_hbm, sv_hbm))
    ]
    table_copies = [
        pltpu.make_async_copy(
            table_hbm.at[:, jnp.where(half == 0, s, 15 - s) if half else s, :, k],
            tab.at[:, half],
            tab_sem.at[half],
        )
        for half in range(2)
    ]
    for copy in weight_copies + table_copies:
        copy.start()

    gain = gain_ref[...].astype(F32)
    xg[:, z] = normalized(stream_ref[...].astype(F32), gain)

    partners = [(s, sib), (s, up_c), (s, down_c), (other_s, c)]
    for d in range(1, 4):
        peer = y * 4 + (x + d) % 4
        partners += [(peer, c), (peer, sib)]
    greet(partners)

    def own_copies(jj):
        rows = pl.ds(2 * jj, 2)
        return [
            remote(xg.at[rows, z], xg.at[rows, z], own_s.at[jj, d], own_r.at[jj, d], s, target)
            for d, target in ((0, up_c), (1, down_c))
        ]

    def own_wait(jj):
        rows = pl.ds(2 * jj, 2)
        arrived(xg.at[rows, down], own_r.at[jj, 0])
        arrived(xg.at[rows, up], own_r.at[jj, 1])

    def relay_copies(jj):
        made = []
        for d, source, target in ((0, down, up_c), (1, up, down_c)):
            row = 2 * jj + d
            made.append(
                remote(
                    xg.at[row, source], xg.at[row, source],
                    relay_s.at[jj, d], relay_r.at[jj, d], s, target,
                )
            )
        return made

    def relay_wait(jj):
        for d in range(2):
            arrived(xg.at[2 * jj + d, far], relay_r.at[jj, d])

    core_of_rows = x // 2

    def q_sends(jj, d):
        hx = (x + d) % 4
        rows = pl.ds(4 * jj, 4)
        src = qst.at[jj, hx]
        dst = q_out.at[rows, x % 2, :, k]
        recv = q_r.at[jj, x % 2, k]
        far_copy = remote(src, dst, q_s.at[jj, d], recv, y * 4 + hx, z * 2 + core_of_rows)
        near_copy = pltpu.make_async_copy(src, dst, recv)
        return far_copy, near_copy

    def kv_send(jj, d):
        hx = (x + d) % 4
        rows = pl.ds(4 * jj, 4)
        src = kvst.at[jj, hx]
        dst = kv_out.at[rows, s, :, k]
        recv = kv_r.at[jj, x]
        if d == 0:
            return pltpu.make_async_copy(src, dst, recv)
        return remote(src, dst, kv_s.at[jj, d], recv, y * 4 + hx, c)

    def y_forward(jj, d):
        a = y * 4 + (x + d) % 4
        rows = pl.ds(4 * jj, 4)
        part = kv_out.at[rows, a, :, k]
        src = kvst.at[jj, x] if d == 0 else part
        return remote(src, part, yf_s.at[jj, d], yf_r.at[jj, (x + d) % 4], other_s, c)

    def core_forward(jj, which):
        first = y * 4 if which == 0 else (1 - y) * 4
        part = kv_out.at[pl.ds(4 * jj, 4), pl.ds(first, 4), :, k]
        send, recv = (f1_s, f1_r) if which == 0 else (f2_s, f2_r)
        return remote(part, part, send.at[jj], recv.at[jj], s, sib)

    def rope(values, cosine, sine):
        return values * cosine + pltpu.roll(values, HEAD_DIM // 2, 1) * sine

    def compute(jj):
        rows = pl.ds(2 * jj, 2)
        lhs = xg[rows].reshape(128, xg.shape[-1])
        trig = tab[rows].reshape(128, 2 * HEAD_DIM)
        cosine, sine = trig[:, :HEAD_DIM], trig[:, HEAD_DIM:]
        for part in range(2):
            core = k if part == 0 else 1 - k
            if jj == 0:
                for i in range(3):
                    weight_copies[3 * part + i].wait()
            qf = jnp.dot(lhs, w[3 * part], preferred_element_type=F32)
            kf = jnp.dot(lhs, w[3 * part + 1], preferred_element_type=F32)
            vf = jnp.dot(lhs, w[3 * part + 2], preferred_element_type=F32)
            for hh in range(2):
                cols = slice(hh * HEAD_DIM, (hh + 1) * HEAD_DIM)
                hx = 2 * core + hh
                qst[jj, hx] = rope(qf[:, cols], cosine, sine).astype(BF16).reshape(4, 2, 16, HEAD_DIM)
                kvst[jj, hx, :, :, :, :HEAD_DIM] = (
                    rope(kf[:, cols], cosine, sine).astype(BF16).reshape(4, 2, 16, HEAD_DIM)
                )
                kvst[jj, hx, :, :, :, HEAD_DIM:] = vf[:, cols].astype(BF16).reshape(4, 2, 16, HEAD_DIM)

    def send_out(jj):
        for d in (2, 1, 3, 0):
            kv_send(jj, d).start()
            if d == 0:
                y_forward(jj, 0).start()
        for d in (2, 1, 3, 0):
            far_copy, near_copy = q_sends(jj, d)
            if d == 0:

                @pl.when(core_of_rows == k)
                def _():
                    near_copy.start()

                @pl.when(core_of_rows != k)
                def _():
                    far_copy.start()
            else:
                far_copy.start()

    def forward_one(jj):
        rows = pl.ds(4 * jj, 4)
        for d in (1, 3, 2, 0):
            a = y * 4 + (x + d) % 4
            arrived(kv_out.at[rows, a, :, k], kv_r.at[jj, (x + d) % 4])
            if d:
                y_forward(jj, d).start()
        core_forward(jj, 0).start()

    def forward_two(jj):
        rows = pl.ds(4 * jj, 4)
        for xs in range(4):
            arrived(kv_out.at[rows, (1 - y) * 4 + xs, :, k], yf_r.at[jj, xs])
        core_forward(jj, 1).start()

    def start_own(jj):
        for copy in own_copies(jj):
            copy.start()

    def start_relay(jj):
        own_wait(jj)
        for copy in relay_copies(jj):
            copy.start()

    start_own(0)
    start_own(1)
    for copy in table_copies:
        copy.wait()
    start_relay(0)
    start_own(2)
    start_relay(1)
    start_own(3)
    relay_wait(0)
    compute(0)
    send_out(0)
    start_relay(2)
    relay_wait(1)
    compute(1)
    send_out(1)
    start_relay(3)
    forward_one(0)
    relay_wait(2)
    compute(2)
    send_out(2)
    forward_one(1)
    relay_wait(3)
    compute(3)
    send_out(3)
    forward_two(0)
    forward_one(2)
    forward_two(1)
    forward_one(3)
    forward_two(2)
    forward_two(3)

    for jj in range(4):
        rows = pl.ds(4 * jj, 4)
        for copy in own_copies(jj) + relay_copies(jj):
            copy.wait_send()
        for d in range(4):
            if d:
                kv_send(jj, d).wait_send()
            y_forward(jj, d).wait_send()
            far_copy, near_copy = q_sends(jj, d)
            if d == 0:

                @pl.when(core_of_rows != k)
                def _():
                    far_copy.wait_send()
            else:
                far_copy.wait_send()
        for which in range(2):
            core_forward(jj, which).wait_send()
        for aa in range(2):
            for kk in range(2):
                arrived(q_out.at[rows, aa, :, kk], q_r.at[jj, aa, kk])
        arrived(kv_out.at[rows, pl.ds(y * 4, 4), :, 1 - k], f1_r.at[jj])
        arrived(kv_out.at[rows, pl.ds((1 - y) * 4, 4), :, 1 - k], f2_r.at[jj])


def attention_kernel(info_ref, q_ref, kv_ref, out_ref, *, chunks, tile):
    log2e = 1.4426950408889634
    factor = HEAD_DIM ** (-0.5) * log2e
    half_rows = tile // 4
    first_block = info_ref[3]

    def row_start(position):
        start = jnp.zeros_like(position)
        for d in range(3):
            start = jnp.where(info_ref[d] <= position, info_ref[d], start)
        return start

    def low_first(g):
        return g * (2 * tile) + first_block * 64

    def high_first(g):
        return g * (2 * tile) + (14 - first_block) * 64

    def low_positions(g):
        row = lax.broadcasted_iota(jnp.int32, (128, 1), 0)
        return low_first(g) + row

    def high_positions(g):
        row = lax.broadcasted_iota(jnp.int32, (128, 1), 0)
        return high_first(g) + jnp.where(row < 64, row + 64, row - 64)

    def key_positions(t):
        col = lax.broadcasted_iota(jnp.int32, (1, tile), 1)
        flipped = (tile // 64 - 1 - col // 64) * 64 + col % 64
        return t * tile + jnp.where(t % 2 == 0, col, flipped)

    def update(state, queries, t, allowed):
        highest, total, weighted = state
        keys = kv_ref[t, :, :HEAD_DIM]
        scores = lax.dot_general(
            queries, keys, (((1,), (1,)), ((), ())), preferred_element_type=F32
        ) * factor
        if allowed is not None:
            scores = jnp.where(allowed, scores, NEGATIVE)
        new_highest = jnp.maximum(highest, jnp.max(scores, axis=1, keepdims=True))
        weights = jnp.exp2(scores - new_highest)
        if allowed is not None:
            weights = jnp.where(allowed, weights, 0.0)
        rescale = jnp.exp2(highest - new_highest)
        total = total * rescale + jnp.sum(weights, axis=1, keepdims=True)
        weighted = weighted * rescale + jnp.dot(
            weights.astype(BF16), kv_ref[t, :, HEAD_DIM:], preferred_element_type=F32
        )
        return new_highest, total, weighted

    def one_chunk(g, carry):
        queries = q_ref[pl.ds(2 * g, 2)].reshape(256, HEAD_DIM)
        positions = jnp.concatenate([low_positions(g), high_positions(g)], axis=0)
        starts = row_start(positions)
        first_tile = row_start(low_first(g)) // tile
        last_start = row_start(high_first(g) + 127)
        plain_tile = jnp.clip((last_start + tile - 1) // tile, first_tile, 2 * g)

        def masked_step(t, state):
            where_keys = key_positions(t)
            allowed = (where_keys <= positions) & (where_keys >= starts)
            return update(state, queries, t, allowed)

        def plain_step(t, state):
            return update(state, queries, t, None)

        state = (
            jnp.full((256, 1), NEGATIVE, F32),
            jnp.zeros((256, 1), F32),
            jnp.zeros((256, HEAD_DIM), F32),
        )
        state = lax.fori_loop(first_tile, plain_tile, masked_step, state)
        state = lax.fori_loop(plain_tile, 2 * g, plain_step, state)
        highest, total, weighted = masked_step(2 * g, state)
        out_ref[2 * g] = (weighted[:128] / total[:128]).astype(BF16)
        t = 2 * g + 1
        where_keys = key_positions(t)
        allowed = (where_keys <= positions[128:]) & (where_keys >= starts[128:])
        highest, total, weighted = update(
            (highest[128:], total[128:], weighted[128:]), queries[128:], t, allowed
        )
        out_ref[t] = (weighted / total).astype(BF16)
        return carry

    lax.fori_loop(0, chunks, one_chunk, 0)


def out_kernel(
    ctx_ref, stream_ref, o_hbm, so_hbm,
    out_ref,
    cbuf, w, mine, zsend, zrecv,
    w_sem, x_s, x_r, zsem_s, zsem_r,
):
    s, c, y, x, z, k = place()
    sib = c + 1 - 2 * k
    weight_copies = [
        pltpu.make_async_copy(src, w.at[i], w_sem.at[i]) for i, src in enumerate((o_hbm, so_hbm))
    ]
    for copy in weight_copies:
        copy.start()
    ring = RingSum(zsend, zrecv, zsem_s, zsem_r, s, z, k)
    partners = [(s, sib), (s, ring.up_c), (s, ring.down_c)]
    for d in range(1, 4):
        peer = y * 4 + (x + d) % 4
        partners += [(peer, c), (peer, sib)]
    greet(partners)

    def x_copies(jj, aa, kk):
        target_x = 2 * k + aa
        src = ctx_ref.at[pl.ds(4 * jj, 4), aa, :, kk]
        dst = cbuf.at[x, pl.ds(4 * jj, 4)]
        recv = x_r.at[jj, x]
        far_copy = remote(src, dst, x_s.at[jj, aa, kk], recv, y * 4 + target_x, z * 2 + kk)
        near_copy = pltpu.make_async_copy(src, dst, recv)
        return far_copy, near_copy, (target_x == x) & (k == kk)

    for jj in range(4):
        for aa in range(2):
            for kk in range(2):
                far_copy, near_copy, here = x_copies(jj, aa, kk)

                @pl.when(here)
                def _():
                    near_copy.start()

                @pl.when(jnp.logical_not(here))
                def _():
                    far_copy.start()

    width = w.shape[-1]
    cols_n = 512

    def compute(jj):
        rows = pl.ds(4 * jj, 4)
        for xs in range(4):
            arrived(cbuf.at[xs, rows], x_r.at[jj, xs])
        if jj == 0:
            for copy in weight_copies:
                copy.wait()

        def side(core):
            return jnp.concatenate(
                [cbuf[2 * core + hh, rows].reshape(128, HEAD_DIM) for hh in range(2)], axis=1
            )

        own, other = side(k), side(1 - k)

        @pl.loop(0, width // cols_n)
        def _(n):
            cols = pl.ds(pl.multiple_of(n * cols_n, cols_n), cols_n)
            part = jnp.dot(own, w[0, :, cols], preferred_element_type=F32)
            part += jnp.dot(other, w[1, :, cols], preferred_element_type=F32)
            mine[jj, :, :, :, cols] = part.reshape(2, 4, 16, cols_n)

    def piece(jj):
        def value(zd, t):
            return mine[jj, t, zd]

        return value

    def third(jj):
        totals = ring.third(jj, piece(jj))
        for t in range(2):
            g = 2 * jj + t
            out_ref[g] = (totals[t] + stream_ref[g].astype(F32)).astype(BF16)

    compute(0)
    ring.first(0, piece(0))
    compute(1)
    ring.first(1, piece(1))
    ring.second(0, piece(0))
    compute(2)
    ring.first(2, piece(2))
    ring.second(1, piece(1))
    compute(3)
    ring.first(3, piece(3))
    third(0)
    ring.second(2, piece(2))
    third(1)
    ring.second(3, piece(3))
    third(2)
    third(3)

    for jj in range(4):
        ring.finish(jj)
        for aa in range(2):
            for kk in range(2):
                far_copy, near_copy, here = x_copies(jj, aa, kk)

                @pl.when(jnp.logical_not(here))
                def _():
                    far_copy.wait_send()


ANY = pl.BlockSpec(memory_space=pl.ANY)
VM = pl.BlockSpec(memory_space=pltpu.VMEM)
SM = pl.BlockSpec(memory_space=pltpu.SMEM)
DMA = pltpu.SemaphoreType.DMA


def params(collective_id):
    return pltpu.CompilerParams(
        collective_id=collective_id, has_side_effects=True, vmem_limit_bytes=VMEM_LIMIT
    )


def like(array):
    return jax.ShapeDtypeStruct(array.shape, array.dtype)


def feed_forward(tokens, gain, gate, up, down, query, key, value, out):
    rows, width = tokens.shape
    ff = gate.shape[1]
    return pl.pallas_call(
        ff_kernel,
        name="feed_forward",
        out_shape=[
            jax.ShapeDtypeStruct((8, 16, width), BF16), like(query), like(key), like(value), like(out),
        ],
        in_specs=[ANY, VM] + [ANY] * 7,
        out_specs=[ANY] * 5,
        scratch_shapes=[
            pltpu.VMEM((rows, width), BF16),
            pltpu.VMEM((width, ff), BF16),
            pltpu.VMEM((width, ff), BF16),
            pltpu.VMEM((ff, width), BF16),
            pltpu.VMEM((256, width), BF16),
            pltpu.VMEM((256, ff), BF16),
            pltpu.VMEM((4, 4, 2, 16, width), F32),
            pltpu.VMEM((4, 4, 2, 16, width), BF16),
            pltpu.VMEM((4, 4, 2, 16, width), BF16),
            pltpu.VMEM((4, 2, 3, 16, width), BF16),
            pltpu.VMEM((4, 2, 3, 16, width), BF16),
            pltpu.VMEM((4, 2, 16, width), BF16),
            DMA((4, 2)), DMA((4, 2)), DMA((1,)), DMA((4,)), DMA((4,)), DMA((4,)), DMA((4,)),
            DMA((4, 2, 2)), DMA((4, 2, 2)), DMA((4, 2)), DMA((8,)), DMA((1,)),
        ],
        compiler_params=params(1),
    )(tokens, gain.reshape(1, width), gate, up, down, query, key, value, out)


def project(stream, gain, own, other, table):
    width = stream.shape[-1]
    cols = own[0].shape[1]
    return pl.pallas_call(
        qkv_kernel,
        name="project",
        out_shape=[
            jax.ShapeDtypeStruct((16, 2, 2, 2, 16, HEAD_DIM), BF16),
            jax.ShapeDtypeStruct((16, 8, 2, 2, 16, 2 * HEAD_DIM), BF16),
        ],
        in_specs=[VM, VM] + [ANY] * 7,
        out_specs=[ANY] * 2,
        scratch_shapes=[
            pltpu.VMEM((8, 4, 16, width), BF16),
            pltpu.VMEM((6, width, cols), BF16),
            pltpu.VMEM((8, 2, 2, 16, 2 * HEAD_DIM), F32),
            pltpu.VMEM((4, 4, 4, 2, 16, HEAD_DIM), BF16),
            pltpu.VMEM((4, 4, 4, 2, 16, 2 * HEAD_DIM), BF16),
            DMA((6,)), DMA((2,)),
            DMA((4, 2)), DMA((4, 2)), DMA((4, 2)), DMA((4, 2)),
            DMA((4, 4)), DMA((4, 2, 2)), DMA((4, 4)), DMA((4, 4)),
            DMA((4, 4)), DMA((4, 4)), DMA((4,)), DMA((4,)), DMA((4,)), DMA((4,)),
        ],
        compiler_params=params(2),
    )(stream, gain.reshape(1, width), *own, *other, table)


def attend(info, queries, keys_values):
    tiles = keys_values.shape[0]
    tile = keys_values.shape[1]
    return pl.pallas_call(
        functools.partial(attention_kernel, chunks=tiles // 2, tile=tile),
        name="attend",
        out_shape=like(queries),
        in_specs=[SM, VM, VM],
        out_specs=VM,
        compiler_params=pltpu.CompilerParams(vmem_limit_bytes=VMEM_LIMIT),
    )(info, queries, keys_values)


def merge(context, stream, own, other):
    width = stream.shape[-1]
    return pl.pallas_call(
        out_kernel,
        name="merge",
        out_shape=like(stream),
        in_specs=[ANY, VM, ANY, ANY],
        out_specs=VM,
        scratch_shapes=[
            pltpu.VMEM((4, 16, 2, 16, HEAD_DIM), BF16),
            pltpu.VMEM((2,) + own.shape, BF16),
            pltpu.VMEM((4, 2, 4, 16, width), F32),
            pltpu.VMEM((4, 2, 3, 16, width), BF16),
            pltpu.VMEM((4, 2, 3, 16, width), BF16),
            DMA((2,)), DMA((4, 2, 2)), DMA((4, 4)), DMA((4, 2, 2)), DMA((4, 2, 2)),
        ],
        compiler_params=params(3),
    )(context, stream, own, other)


def body(
    tokens, doc_ids, mlp_gain, gate_weight, up_weight, down_weight,
    attn_gain, query_weight, key_weight, value_weight, out_weight,
):
    s = lax.axis_index("seq")
    k = lax.axis_index("tensor") % 2
    starts = jnp.sum(
        (doc_ids[None, :] < jnp.arange(1, 4, dtype=jnp.int32)[:, None]).astype(jnp.int32), axis=1
    )
    first_block = (s // 4) * 4 + 2 * k
    info = jnp.concatenate([starts, first_block[None].astype(jnp.int32)])
    stream, sq, sk, sv, so = feed_forward(
        tokens, mlp_gain, gate_weight, up_weight, down_weight,
        query_weight, key_weight, value_weight, out_weight,
    )
    table = jnp.asarray(rope_table(8, tokens.shape[0]))
    queries, keys_values = project(
        stream, attn_gain, (query_weight, key_weight, value_weight), (sq, sk, sv), table
    )
    context = attend(
        info, queries.reshape(16, 128, HEAD_DIM), keys_values.reshape(16, 512, 2 * HEAD_DIM)
    )
    merged = merge(context.reshape(16, 2, 2, 2, 16, HEAD_DIM), stream, out_weight, so)
    return merged.reshape(128, tokens.shape[1])


def solution(mesh):
    in_specs = (
        P(("dp", "seq"), None),
        P("dp"),
        P(),
        P(None, "tensor"),
        P(None, "tensor"),
        P("tensor", None),
        P(),
        P(None, "tensor"),
        P(None, "tensor"),
        P(None, "tensor"),
        P("tensor", None),
    )
    out_specs = P(("dp", "seq", "tensor"), None)
    return jax.shard_map(body, mesh=mesh, in_specs=in_specs, out_specs=out_specs, check_vma=False)
```

```python
import functools

import jax
import jax.numpy as jnp
import numpy as np
from jax import lax
from jax.experimental import pallas as pl
from jax.experimental.pallas import tpu as pltpu
from jax.sharding import PartitionSpec as P

HEAD_DIM = 128
EPSILON = 1e-05
ROPE_BASE = 500000.0
NEGATIVE = -1e30
MESH = pl.DeviceIdType.MESH
F32 = jnp.float32
BF16 = jnp.bfloat16
VMEM_LIMIT = 60 * 1024 * 1024


def place():
    s = lax.axis_index("seq")
    c = lax.axis_index("tensor")
    return s, c, s // 4, s % 4, c // 2, c % 2


def remote(src, dst, send_sem, recv_sem, seq, tensor):
    return pltpu.make_async_remote_copy(
        src_ref=src,
        dst_ref=dst,
        send_sem=send_sem,
        recv_sem=recv_sem,
        device_id={"dp": lax.axis_index("dp"), "seq": seq, "tensor": tensor},
        device_id_type=MESH,
    )


def arrived(dst, recv_sem):
    pltpu.make_async_copy(dst, dst, recv_sem).wait()


def greet_signal(partners):
    barrier = pltpu.get_barrier_semaphore()
    for seq, tensor in partners:
        pl.semaphore_signal(
            barrier,
            inc=1,
            device_id={"dp": lax.axis_index("dp"), "seq": seq, "tensor": tensor},
            device_id_type=MESH,
        )


def greet_wait(partners):
    pl.semaphore_wait(pltpu.get_barrier_semaphore(), len(partners))


def greet(partners):
    greet_signal(partners)
    greet_wait(partners)


def normalized(values, gain):
    mean_square = jnp.mean(values * values, axis=-1, keepdims=True)
    gain = gain.reshape((1,) * (values.ndim - 1) + gain.shape)
    return (values * lax.rsqrt(mean_square + EPSILON) * gain).astype(BF16)


class RingSum:
    def __init__(self, send, recv, send_sem, recv_sem, s, z, k):
        self.send, self.recv = send, recv
        self.send_sem, self.recv_sem = send_sem, recv_sem
        self.s, self.z = s, z
        self.up = (z + 1) % 4
        self.down = (z + 3) % 4
        self.far = (z + 2) % 4
        self.up_c = self.up * 2 + k
        self.down_c = self.down * 2 + k

    def copies(self, ch, phase):
        part = pl.ds(0, 2) if phase == 0 else pl.ds(2, 1)
        made = []
        for d, target in ((0, self.up_c), (1, self.down_c)):
            made.append(
                remote(
                    self.send.at[ch, d, part],
                    self.recv.at[ch, d, part],
                    self.send_sem.at[ch, d, phase],
                    self.recv_sem.at[ch, d, phase],
                    self.s,
                    target,
                )
            )
        return made

    def first(self, ch, value):
        self.send[ch, 0, 0] = value(self.far, 0).astype(BF16)
        self.send[ch, 0, 1] = value(self.up, 1).astype(BF16)
        self.send[ch, 1, 0] = value(self.far, 1).astype(BF16)
        self.send[ch, 1, 1] = value(self.down, 0).astype(BF16)
        for copy in self.copies(ch, 0):
            copy.start()

    def second(self, ch, value):
        for copy in self.copies(ch, 0):
            copy.wait_recv()
        self.send[ch, 0, 2] = (value(self.up, 0) + self.recv[ch, 0, 0].astype(F32)).astype(BF16)
        self.send[ch, 1, 2] = (value(self.down, 1) + self.recv[ch, 1, 0].astype(F32)).astype(BF16)
        for copy in self.copies(ch, 1):
            copy.start()

    def third(self, ch, value):
        for copy in self.copies(ch, 1):
            copy.wait_recv()
        one = (
            value(self.z, 0)
            + self.recv[ch, 0, 2].astype(F32)
            + self.recv[ch, 1, 1].astype(F32)
        )
        two = (
            value(self.z, 1)
            + self.recv[ch, 0, 1].astype(F32)
            + self.recv[ch, 1, 2].astype(F32)
        )
        return one, two

    def finish(self, ch):
        for phase in range(2):
            for copy in self.copies(ch, phase):
                copy.wait_send()


def rope_table(groups, base_rows):
    half = HEAD_DIM // 2
    frequency = ROPE_BASE ** (-(np.arange(half, dtype=np.float64) / half))
    angles = np.arange(groups * base_rows, dtype=np.float64)[:, None] * frequency[None, :]
    cosine, sine = np.cos(angles), np.sin(angles)
    table = np.concatenate([cosine, cosine, -sine, sine], axis=1).astype(np.float32)
    return table.reshape(groups, 16, 2, 2, 16, 4 * half)


ORDER = (
    "H0", "G0", "D0", "H1", "A0", "D1", "W1", "H2", "A1", "D2", "W2", "H3", "B0", "A2", "D3", "B1",
    "C0", "A3", "W3", "B2", "C1", "N0", "B3", "C2", "N1", "C3", "R0", "N2", "W4", "R1", "N3", "Q0",
    "R2", "Q1", "F0", "Q2", "R3", "F1", "Q3", "W5", "E0", "F2", "E1", "F3", "E2", "E3",
)


GATHERS = 15


def front_kernel(
    tok_hbm, mlp_gain_ref, wg_hbm, wu_hbm, wd_hbm, attn_gain_ref, q_hbm, k_hbm, v_hbm, o_hbm, table_hbm,
    stream_ref, q_out, kv_out, wo_out,
    tok, wg, wu, wd, xn, hid, mine, csend, crecv, zsend, zrecv, sstage, xg, w, tab, qst, kvst,
    tok_sem, gu_sem, wd_sem, wsem_s, wsem_r, csem_s, csem_r, zsem_s, zsem_r, ssem_s, ssem_r,
    w_sem, tab_sem, own_s, own_r, relay_s, relay_r, q_s, q_r, kv_s, kv_r, yf_s, yf_r,
    f1_s, f1_r, f2_s, f2_r, g_s, g_r,
):
    s, c, y, x, z, k = place()
    sib = c + 1 - 2 * k
    ff = wg.shape[1]
    width = tok.shape[1]
    gu_tiles = 4
    gu_cols = ff // gu_tiles
    up, down, far = (z + 1) % 4, (z + 3) % 4, (z + 2) % 4
    up_c, down_c = up * 2 + k, down * 2 + k
    other_s = (1 - y) * 4 + x
    core_of_rows = x // 2

    def pair_of(ch):
        return (s // 2 + 1 + ch) % 4

    def source_of(ch, pair):
        return (pair + 3 - ch) % 4

    def tok_copies(ch):
        a = pair_of(ch) * 2
        low = pl.ds(pl.multiple_of(a * 64, 128), 128)
        high = pl.ds(pl.multiple_of((14 - a) * 64, 128), 128)
        return [
            pltpu.make_async_copy(tok_hbm.at[low], tok.at[low], tok_sem.at[ch, 0]),
            pltpu.make_async_copy(tok_hbm.at[high], tok.at[high], tok_sem.at[ch, 1]),
        ]

    def gu_copies(n):
        cols = pl.ds(n * gu_cols, gu_cols)
        return [
            pltpu.make_async_copy(wg_hbm.at[:, cols], wg.at[:, cols], gu_sem.at[n, 0]),
            pltpu.make_async_copy(wu_hbm.at[:, cols], wu.at[:, cols], gu_sem.at[n, 1]),
        ]

    wd_copy = pltpu.make_async_copy(wd_hbm, wd, wd_sem.at[0])
    own_weights = [
        pltpu.make_async_copy(src, w.at[i], w_sem.at[i]) for i, src in enumerate((q_hbm, k_hbm, v_hbm))
    ]
    table_copies = [
        pltpu.make_async_copy(
            table_hbm.at[:, 15 - s if half else s, :, k], tab.at[:, half], tab_sem.at[half]
        )
        for half in range(2)
    ]
    weight_sends = [
        remote(src, dst, wsem_s.at[i], wsem_r.at[i], s, sib)
        for i, (src, dst) in enumerate(
            ((q_hbm, w.at[3]), (k_hbm, w.at[4]), (v_hbm, w.at[5]))
        )
    ]

    partners = [(s, sib), (s, up_c), (s, down_c)]
    partners += [((s + d) % 8, c) for d in range(1, 8)]
    partners += [(y * 4 + (x + d) % 4, sib) for d in range(1, 4)]
    for copy in tok_copies(0):
        copy.start()
    for n in range(gu_tiles):
        for copy in gu_copies(n):
            copy.start()
    greet_signal(partners)
    wd_copy.start()
    for ch in range(1, 4):
        for copy in tok_copies(ch):
            copy.start()
    for copy in own_weights + table_copies:
        copy.start()

    def token_rows(ch):
        a = pair_of(ch) * 2
        low = tok[pl.ds(pl.multiple_of(a * 64, 128), 128), :]
        high = tok[pl.ds(pl.multiple_of((14 - a) * 64, 128), 128), :]
        return low, high

    def step_H(ch):
        for copy in tok_copies(ch):
            copy.wait()
        low, high = token_rows(ch)
        gain = mlp_gain_ref[...].astype(F32)
        xn[0:128, :] = normalized(low.astype(F32), gain)
        xn[128:256, :] = normalized(high.astype(F32), gain)
        for n in range(gu_tiles):
            if ch == 0:
                for copy in gu_copies(n):
                    copy.wait()
            cols = slice(n * gu_cols, (n + 1) * gu_cols)
            gate = jnp.dot(xn[...], wg[:, cols], preferred_element_type=F32)
            up_part = jnp.dot(xn[...], wu[:, cols], preferred_element_type=F32)
            hid[:, cols] = (gate / (1.0 + jnp.exp(-gate)) * up_part).astype(BF16)

    def core_copy(ch):
        return remote(csend.at[ch], crecv.at[ch], csem_s.at[ch], csem_r.at[ch], s, sib)

    def step_G(ch):
        greet_wait(partners)
        for copy in weight_sends:
            copy.start()
        gather_own().start()
        for d in range(2):
            gather(d).start()

    def step_D(ch):
        if ch == 0:
            wd_copy.wait()
        cols_n = 256
        for n in range(width // cols_n):
            cols = slice(n * cols_n, (n + 1) * cols_n)
            part = jnp.dot(hid[...], wd[:, cols], preferred_element_type=F32)
            part = part.reshape(4, 2, 2, 16, cols_n)
            even, odd = part[:, :, 0], part[:, :, 1]
            mine[ch, :, :, :, cols] = jnp.where(k == 0, even, odd)
            csend[ch, :, :, :, cols] = jnp.where(k == 0, odd, even).astype(BF16)
        core_copy(ch).start()

    x_up, x_down, x_far = (x + 1) % 4, (x + 3) % 4, (x + 2) % 4
    slice_rows = o_hbm.shape[0] // 8

    def gather_own():
        mine_rows = o_hbm.at[pl.ds(pl.multiple_of(slice_rows * s, slice_rows), slice_rows)]
        return pltpu.make_async_copy(mine_rows, wo_out.at[z, k, y, x], g_r.at[GATHERS])

    def gather(i):
        half = slice_rows // 2
        if i < 2:
            src = o_hbm.at[pl.ds(pl.multiple_of(slice_rows * s, slice_rows), slice_rows)]
            dst, to = wo_out.at[z, k, y, x], (s, up_c if i == 0 else down_c)
        elif i < 4:
            d = i - 2
            dst = wo_out.at[up if d else down, k, y, x, pl.ds(d * half, half)]
            src, to = dst, (s, down_c if d else up_c)
        elif i == 4:
            dst = wo_out.at[:, k, y, x]
            src, to = dst, (other_s, c)
        elif i < 9:
            d = (i - 5) % 2
            dst = wo_out.at[:, k, y if i < 7 else 1 - y, x]
            src, to = dst, (y * 4 + (x_down if d else x_up), c)
        elif i < 11:
            d = i - 9
            dst = wo_out.at[pl.ds(2 * d, 2), k, :, x_up if d else x_down]
            src, to = dst, (y * 4 + (x_down if d else x_up), c)
        else:
            dst = wo_out.at[:, k, :, (x, x_up, x_down, x_far)[i - 11]]
            src, to = dst, (s, sib)
        return remote(src, dst, g_s.at[i], g_r.at[i], *to)

    def gather_wait(i):
        half = slice_rows // 2
        if i < 2:
            dst = wo_out.at[up if i else down, k, y, x]
        elif i < 4:
            dst = wo_out.at[far, k, y, x, pl.ds((i - 2) * half, half)]
        elif i == 4:
            dst = wo_out.at[:, k, 1 - y, x]
        elif i < 9:
            dst = wo_out.at[:, k, y if i < 7 else 1 - y, x_up if (i - 5) % 2 else x_down]
        elif i < 11:
            dst = wo_out.at[pl.ds(2 * (i - 9), 2), k, :, x_far]
        else:
            dst = wo_out.at[:, 1 - k, :, (x, x_up, x_down, x_far)[i - 11]]
        arrived(dst, g_r.at[i])

    def step_W(i):
        waits, starts = (
            ((0, 1), (2, 3)),
            ((2, 3), (4, 5, 6)),
            ((4,), (7, 8, 11)),
            ((5, 6, 7, 8), (9, 10, 12, 13)),
            ((9, 10), (14,)),
        )[i - 1]
        if i == 2:
            gather_own().wait()
        for j in waits:
            gather_wait(j)
        for j in starts:
            gather(j).start()

    ring = RingSum(zsend, zrecv, zsem_s, zsem_r, s, z, k)

    def piece(ch):
        def value(zd, t):
            block = jnp.where(zd < 2, t, 3 - t)
            return mine[ch, block, zd % 2] + crecv[ch, block, zd % 2].astype(F32)

        return value

    def step_A(ch):
        core_copy(ch).wait_recv()
        ring.first(ch, piece(ch))

    def step_B(ch):
        ring.second(ch, piece(ch))

    def seq_copy(ch, t, target):
        return remote(
            sstage.at[ch, t], stream_ref.at[s], ssem_s.at[ch, t], ssem_r.at[s], target, c
        )

    def step_C(ch):
        totals = ring.third(ch, piece(ch))
        a = pair_of(ch) * 2
        for t in range(2):
            block = jnp.where(z < 2, a + t, 15 - a - t)
            start = pl.multiple_of(block * 64 + (2 * (z % 2) + k) * 16, 16)
            rows = tok[pl.ds(start, 16), :].astype(F32)
            result = (totals[t] + rows).astype(BF16)
            if ch < 3:
                sstage[ch, t] = result
                seq_copy(ch, t, a + t).start()
            else:

                @pl.when(s == a + t)
                def _():
                    stream_ref[s] = result

                @pl.when(s != a + t)
                def _():
                    sstage[ch, t] = result
                    seq_copy(ch, t, a + t).start()

    def own_copies(ch):
        return [
            remote(xg.at[ch, :, z], xg.at[ch, :, z], own_s.at[ch, d], own_r.at[ch, d], s, target)
            for d, target in ((0, up_c), (1, down_c))
        ]

    def step_N(ch):
        g = 2 * source_of(ch, s // 2)
        if ch < 3:
            for t in range(2):
                arrived(stream_ref.at[g + t], ssem_r.at[g + t])
        else:
            other = g + 1 - s % 2
            arrived(stream_ref.at[other], ssem_r.at[other])
        gain = attn_gain_ref[...].astype(F32)
        xg[ch, :, z] = normalized(stream_ref[pl.ds(g, 2)].astype(F32), gain)
        for copy in own_copies(ch):
            copy.start()

    def relay_copies(ch):
        return [
            remote(
                xg.at[ch, d, source], xg.at[ch, d, source],
                relay_s.at[ch, d], relay_r.at[ch, d], s, target,
            )
            for d, source, target in ((0, down, up_c), (1, up, down_c))
        ]

    def step_R(ch):
        arrived(xg.at[ch, :, down], own_r.at[ch, 0])
        arrived(xg.at[ch, :, up], own_r.at[ch, 1])
        for copy in relay_copies(ch):
            copy.start()

    def out_rows(ch, sy, sx):
        return pl.ds(4 * source_of(ch, 2 * sy + sx // 2), 4)

    def q_far(ch, d):
        hx = (x + d) % 4
        return remote(
            qst.at[ch, hx], q_out.at[out_rows(ch, y, x), x % 2, :, k],
            q_s.at[ch, d], q_r.at[ch, x % 2, k], y * 4 + hx, z * 2 + core_of_rows,
        )

    def q_near(ch):
        return pltpu.make_async_copy(
            qst.at[ch, x], q_out.at[out_rows(ch, y, x), x % 2, :, k], q_r.at[ch, x % 2, k]
        )

    def kv_send(ch, d):
        hx = (x + d) % 4
        src = kvst.at[ch, hx]
        dst = kv_out.at[out_rows(ch, y, x), s, :, k]
        if d == 0:
            return pltpu.make_async_copy(src, dst, kv_r.at[ch, x])
        return remote(src, dst, kv_s.at[ch, d], kv_r.at[ch, x], y * 4 + hx, c)

    def y_forward(ch, d):
        sx = (x + d) % 4
        part = kv_out.at[out_rows(ch, y, sx), y * 4 + sx, :, k]
        src = kvst.at[ch, x] if d == 0 else part
        return remote(src, part, yf_s.at[ch, d], yf_r.at[ch, sx], other_s, c)

    def core_forwards(ch, which):
        sy = y if which == 0 else 1 - y
        send, recv = (f1_s, f1_r) if which == 0 else (f2_s, f2_r)
        made = []
        for h in range(2):
            part = kv_out.at[out_rows(ch, sy, 2 * h), pl.ds(sy * 4 + 2 * h, 2), :, k]
            made.append(remote(part, part, send.at[ch, h], recv.at[ch, h], s, sib))
        return made

    def rope(values, cosine, sine):
        return values * cosine + pltpu.roll(values, HEAD_DIM // 2, 1) * sine

    def step_Q(ch):
        for d in range(2):
            arrived(xg.at[ch, d, far], relay_r.at[ch, d])
        if ch == 0:
            for copy in own_weights + table_copies:
                copy.wait()
            for i, copy in enumerate(weight_sends):
                copy.wait_recv()
        lhs = xg[ch].reshape(128, width)
        trig = tab[pl.ds(2 * source_of(ch, s // 2), 2)].reshape(128, 2 * HEAD_DIM)
        cosine, sine = trig[:, :HEAD_DIM], trig[:, HEAD_DIM:]
        for part in range(2):
            core = k if part == 0 else 1 - k
            kf = jnp.dot(lhs, w[3 * part + 1], preferred_element_type=F32)
            vf = jnp.dot(lhs, w[3 * part + 2], preferred_element_type=F32)
            qf = jnp.dot(lhs, w[3 * part], preferred_element_type=F32)
            for hh in range(2):
                cols = slice(hh * HEAD_DIM, (hh + 1) * HEAD_DIM)
                hx = 2 * core + hh
                qst[ch, hx] = rope(qf[:, cols], cosine, sine).astype(BF16).reshape(4, 2, 16, HEAD_DIM)
                kvst[ch, hx, :, :, :, :HEAD_DIM] = (
                    rope(kf[:, cols], cosine, sine).astype(BF16).reshape(4, 2, 16, HEAD_DIM)
                )
                kvst[ch, hx, :, :, :, HEAD_DIM:] = vf[:, cols].astype(BF16).reshape(4, 2, 16, HEAD_DIM)
        for d in (2, 1, 3, 0):
            kv_send(ch, d).start()
        y_forward(ch, 0).start()
        for d in (2, 1, 3):
            q_far(ch, d).start()

        @pl.when(core_of_rows == k)
        def _():
            q_near(ch).start()

        @pl.when(core_of_rows != k)
        def _():
            q_far(ch, 0).start()

    def step_F(ch):
        for d in (1, 3, 2, 0):
            sx = (x + d) % 4
            arrived(kv_out.at[out_rows(ch, y, sx), y * 4 + sx, :, k], kv_r.at[ch, sx])
            if d:
                y_forward(ch, d).start()
        for copy in core_forwards(ch, 0):
            copy.start()

    def step_E(ch):
        for sx in range(4):
            arrived(kv_out.at[out_rows(ch, 1 - y, sx), (1 - y) * 4 + sx, :, k], yf_r.at[ch, sx])
        for copy in core_forwards(ch, 1):
            copy.start()

    steps = dict(
        H=step_H, G=step_G, D=step_D, A=step_A, B=step_B, C=step_C, N=step_N, R=step_R, Q=step_Q,
        F=step_F, E=step_E, W=step_W,
    )
    for name in ORDER:
        steps[name[0]](int(name[1]))

    for ch in range(4):
        core_copy(ch).wait_send()
        ring.finish(ch)
        a = pair_of(ch) * 2
        for t in range(2):
            if ch < 3:
                seq_copy(ch, t, a + t).wait_send()
            else:

                @pl.when(s != a + t)
                def _():
                    seq_copy(ch, t, a + t).wait_send()

        for copy in own_copies(ch) + relay_copies(ch):
            copy.wait_send()
        for d in range(4):
            if d:
                kv_send(ch, d).wait_send()
                q_far(ch, d).wait_send()
            y_forward(ch, d).wait_send()

        @pl.when(core_of_rows != k)
        def _():
            q_far(ch, 0).wait_send()

        for which in range(2):
            for copy in core_forwards(ch, which):
                copy.wait_send()
        for aa in range(2):
            sx = 2 * k + aa
            for kk in range(2):
                arrived(q_out.at[out_rows(ch, y, sx), aa, :, kk], q_r.at[ch, aa, kk])
        for h in range(2):
            for sy, recv in ((y, f1_r), (1 - y, f2_r)):
                arrived(
                    kv_out.at[out_rows(ch, sy, 2 * h), pl.ds(sy * 4 + 2 * h, 2), :, 1 - k],
                    recv.at[ch, h],
                )
    for copy in weight_sends:
        copy.wait_send()
    for i in range(GATHERS):
        gather(i).wait_send()
    for i in range(11, GATHERS):
        gather_wait(i)


def attention_kernel(doc_ref, q_ref, kv_ref, out_ref, *, chunks, tile):
    log2e = 1.4426950408889634
    factor = HEAD_DIM ** (-0.5) * log2e
    half_rows = tile // 4
    s, c, y, x, z, k = place()
    first_block = 4 * y + 2 * k
    starts_of = [jnp.sum((doc_ref[...] < d).astype(jnp.int32)) for d in range(1, 4)]

    def row_start(position):
        start = jnp.zeros_like(position)
        for d in range(3):
            start = jnp.where(starts_of[d] <= position, starts_of[d], start)
        return start

    def low_first(g):
        return g * (2 * tile) + first_block * 64

    def high_first(g):
        return g * (2 * tile) + (14 - first_block) * 64

    def low_positions(g):
        row = lax.broadcasted_iota(jnp.int32, (128, 1), 0)
        return low_first(g) + row

    def high_positions(g):
        row = lax.broadcasted_iota(jnp.int32, (128, 1), 0)
        return high_first(g) + jnp.where(row < 64, row + 64, row - 64)

    def key_positions(t):
        col = lax.broadcasted_iota(jnp.int32, (1, tile), 1)
        flipped = (tile // 64 - 1 - col // 64) * 64 + col % 64
        return t * tile + jnp.where(t % 2 == 0, col, flipped)

    def update(state, queries, t, allowed):
        highest, total, weighted = state
        keys = kv_ref[t, :, :HEAD_DIM]
        scores = lax.dot_general(
            queries, keys, (((1,), (1,)), ((), ())), preferred_element_type=F32
        ) * factor
        if allowed is not None:
            scores = jnp.where(allowed, scores, NEGATIVE)
        new_highest = jnp.maximum(highest, jnp.max(scores, axis=1, keepdims=True))
        weights = jnp.exp2(scores - new_highest)
        if allowed is not None:
            weights = jnp.where(allowed, weights, 0.0)
        rescale = jnp.exp2(highest - new_highest)
        total = total * rescale + jnp.sum(weights, axis=1, keepdims=True)
        weighted = weighted * rescale + jnp.dot(
            weights.astype(BF16), kv_ref[t, :, HEAD_DIM:], preferred_element_type=F32
        )
        return new_highest, total, weighted

    def one_chunk(g, carry):
        queries = q_ref[pl.ds(2 * g, 2)].reshape(256, HEAD_DIM)
        positions = jnp.concatenate([low_positions(g), high_positions(g)], axis=0)
        starts = row_start(positions)
        first_tile = row_start(low_first(g)) // tile
        last_start = row_start(high_first(g) + 127)
        plain_tile = jnp.clip((last_start + tile - 1) // tile, first_tile, 2 * g)

        def masked_step(t, state):
            where_keys = key_positions(t)
            allowed = (where_keys <= positions) & (where_keys >= starts)
            return update(state, queries, t, allowed)

        def plain_step(t, state):
            return update(state, queries, t, None)

        state = (
            jnp.full((256, 1), NEGATIVE, F32),
            jnp.zeros((256, 1), F32),
            jnp.zeros((256, HEAD_DIM), F32),
        )
        state = lax.fori_loop(first_tile, plain_tile, masked_step, state)
        state = lax.fori_loop(plain_tile, 2 * g, plain_step, state)
        highest, total, weighted = masked_step(2 * g, state)
        out_ref[2 * g] = (weighted[:128] / total[:128]).astype(BF16)
        t = 2 * g + 1
        where_keys = key_positions(t)
        allowed = (where_keys <= positions[128:]) & (where_keys >= starts[128:])
        highest, total, weighted = update(
            (highest[128:], total[128:], weighted[128:]), queries[128:], t, allowed
        )
        out_ref[t] = (weighted / total).astype(BF16)
        return carry

    lax.fori_loop(0, chunks, one_chunk, 0)


def out_kernel(ctx_ref, stream_ref, wo_hbm, out_ref, cbuf, w, w_sem, x_s, x_r):
    s, c, y, x, z, k = place()
    width = w.shape[1]
    weight_copy = pltpu.make_async_copy(wo_hbm, w, w_sem.at[0])
    weight_copy.start()
    here = x // 2 == k
    barrier = pltpu.get_barrier_semaphore()
    for sx in range(4):
        for sz in range(4):
            seq, tensor = y * 4 + sx, sz * 2 + x // 2

            @pl.when(jnp.logical_not((seq == s) & (tensor == c)))
            def _():
                pl.semaphore_signal(
                    barrier,
                    inc=1,
                    device_id={"dp": lax.axis_index("dp"), "seq": seq, "tensor": tensor},
                    device_id_type=MESH,
                )

    @pl.when(here)
    def _():
        pl.semaphore_wait(barrier, 15)

    @pl.when(jnp.logical_not(here))
    def _():
        pl.semaphore_wait(barrier, 16)

    head = 4 * z + x

    def send(dx, dz, dk):
        aa, tz, tk = (x + dx) % 2, (z + dz) % 4, (k + dk) % 2
        src = ctx_ref.at[:, tz // 2, aa, tz % 2, tk]
        target = y * 4 + 2 * k + aa, tz * 2 + tk
        return src, target

    def far_send(dx, dz, dk):
        src, target = send(dx, dz, dk)
        return remote(src, cbuf.at[head], x_s.at[dx, dz, dk], x_r.at[head], *target)

    def near_send():
        src, _ = send(0, 0, 0)
        return pltpu.make_async_copy(src, cbuf.at[head], x_r.at[head])

    others = [(dx, dz, dk) for dz in (2, 1, 3, 0) for dx in range(2) for dk in range(2)]
    for where in others:
        if where != (0, 0, 0):
            far_send(*where).start()

    @pl.when(here)
    def _():
        near_send().start()

    @pl.when(jnp.logical_not(here))
    def _():
        far_send(0, 0, 0).start()

    weight_copy.wait()
    for h in range(16):
        arrived(cbuf.at[h], x_r.at[h])
    lhs = jnp.concatenate([cbuf[h].reshape(128, HEAD_DIM) for h in range(16)], axis=1)
    cols_n = 256
    for n in range(width // cols_n):
        cols = slice(n * cols_n, (n + 1) * cols_n)
        part = jnp.dot(lhs, w[:, cols], preferred_element_type=F32)
        rows = stream_ref[:, :, cols].astype(F32)
        out_ref[:, :, cols] = (part.reshape(rows.shape) + rows).astype(BF16)

    for where in others:
        if where != (0, 0, 0):
            far_send(*where).wait_send()

    @pl.when(jnp.logical_not(here))
    def _():
        far_send(0, 0, 0).wait_send()


ANY = pl.BlockSpec(memory_space=pl.ANY)
VM = pl.BlockSpec(memory_space=pltpu.VMEM)
SM = pl.BlockSpec(memory_space=pltpu.SMEM)
DMA = pltpu.SemaphoreType.DMA


def params(collective_id):
    return pltpu.CompilerParams(
        collective_id=collective_id, has_side_effects=True, vmem_limit_bytes=VMEM_LIMIT
    )


def like(array):
    return jax.ShapeDtypeStruct(array.shape, array.dtype)


def front(tokens, mlp_gain, gate, up, down, attn_gain, query, key, value, out, table):
    rows, width = tokens.shape
    ff = gate.shape[1]
    cols = query.shape[1]
    return pl.pallas_call(
        front_kernel,
        name="front",
        out_shape=[
            jax.ShapeDtypeStruct((8, 16, width), BF16),
            jax.ShapeDtypeStruct((16, 2, 2, 2, 16, HEAD_DIM), BF16),
            jax.ShapeDtypeStruct((16, 8, 2, 2, 16, 2 * HEAD_DIM), BF16),
            jax.ShapeDtypeStruct((4, 2, 2, 4, out.shape[0] // 8, width), BF16),
        ],
        in_specs=[ANY, VM, ANY, ANY, ANY, VM] + [ANY] * 5,
        out_specs=[VM, ANY, ANY, ANY],
        scratch_shapes=[
            pltpu.VMEM((rows, width), BF16),
            pltpu.VMEM((width, ff), BF16),
            pltpu.VMEM((width, ff), BF16),
            pltpu.VMEM((ff, width), BF16),
            pltpu.VMEM((256, width), BF16),
            pltpu.VMEM((256, ff), BF16),
            pltpu.VMEM((4, 4, 2, 16, width), F32),
            pltpu.VMEM((4, 4, 2, 16, width), BF16),
            pltpu.VMEM((4, 4, 2, 16, width), BF16),
            pltpu.VMEM((4, 2, 3, 16, width), BF16),
            pltpu.VMEM((4, 2, 3, 16, width), BF16),
            pltpu.VMEM((4, 2, 16, width), BF16),
            pltpu.VMEM((4, 2, 4, 16, width), BF16),
            pltpu.VMEM((6, width, cols), BF16),
            pltpu.VMEM((8, 2, 2, 16, 2 * HEAD_DIM), F32),
            pltpu.VMEM((4, 4, 4, 2, 16, HEAD_DIM), BF16),
            pltpu.VMEM((4, 4, 4, 2, 16, 2 * HEAD_DIM), BF16),
            DMA((4, 2)), DMA((4, 2)), DMA((1,)), DMA((3,)), DMA((3,)), DMA((4,)), DMA((4,)),
            DMA((4, 2, 2)), DMA((4, 2, 2)), DMA((4, 2)), DMA((8,)),
            DMA((3,)), DMA((2,)),
            DMA((4, 2)), DMA((4, 2)), DMA((4, 2)), DMA((4, 2)),
            DMA((4, 4)), DMA((4, 2, 2)), DMA((4, 4)), DMA((4, 4)),
            DMA((4, 4)), DMA((4, 4)), DMA((4, 2)), DMA((4, 2)), DMA((4, 2)), DMA((4, 2)),
            DMA((GATHERS,)), DMA((GATHERS + 1,)),
        ],
        compiler_params=params(1),
    )(tokens, mlp_gain, gate, up, down, attn_gain, query, key, value, out, table)


def attend(docs, queries, keys_values):
    tiles = keys_values.shape[0]
    tile = keys_values.shape[1]
    return pl.pallas_call(
        functools.partial(attention_kernel, chunks=tiles // 2, tile=tile),
        name="attend",
        out_shape=like(queries),
        in_specs=[VM, VM, VM],
        out_specs=VM,
        compiler_params=pltpu.CompilerParams(vmem_limit_bytes=VMEM_LIMIT),
    )(docs.reshape(-1, 128), queries, keys_values)


def merge(context, stream, out_weight):
    width = stream.shape[-1]
    return pl.pallas_call(
        out_kernel,
        name="merge",
        out_shape=like(stream),
        in_specs=[ANY, VM, ANY],
        out_specs=VM,
        scratch_shapes=[
            pltpu.VMEM((16, 8, 16, HEAD_DIM), BF16),
            pltpu.VMEM(out_weight.shape, BF16),
            DMA((1,)), DMA((2, 4, 2)), DMA((16,)),
        ],
        compiler_params=params(3),
    )(context, stream, out_weight)


def body(
    tokens, doc_ids, mlp_gain, gate_weight, up_weight, down_weight,
    attn_gain, query_weight, key_weight, value_weight, out_weight,
):
    table = jnp.asarray(rope_table(8, tokens.shape[0]))
    stream, queries, keys_values, whole_out = front(
        tokens, mlp_gain, gate_weight, up_weight, down_weight, attn_gain,
        query_weight, key_weight, value_weight, out_weight, table,
    )
    context = attend(
        doc_ids, queries.reshape(16, 128, HEAD_DIM), keys_values.reshape(16, 512, 2 * HEAD_DIM)
    )
    merged = merge(
        context.reshape(8, 2, 2, 2, 2, 16, HEAD_DIM), stream, whole_out.reshape(-1, tokens.shape[1])
    )
    return merged.reshape(128, tokens.shape[1])


def solution(mesh):
    in_specs = (
        P(("dp", "seq"), None),
        P("dp"),
        P(),
        P(None, "tensor"),
        P(None, "tensor"),
        P("tensor", None),
        P(),
        P(None, "tensor"),
        P(None, "tensor"),
        P(None, "tensor"),
        P("tensor", None),
    )
    out_specs = P(("dp", "seq", "tensor"), None)
    return jax.shard_map(body, mesh=mesh, in_specs=in_specs, out_specs=out_specs, check_vma=False)
```

```python
import functools

import jax
import jax.numpy as jnp
import numpy as np
from jax import lax
from jax.experimental import pallas as pl
from jax.experimental.pallas import tpu as pltpu
from jax.sharding import PartitionSpec as P

HEAD_DIM = 128
EPSILON = 1e-05
ROPE_BASE = 500000.0
NEGATIVE = -1e30
MESH = pl.DeviceIdType.MESH
F32 = jnp.float32
BF16 = jnp.bfloat16
VMEM_LIMIT = 60 * 1024 * 1024


def place():
    s = lax.axis_index("seq")
    c = lax.axis_index("tensor")
    return s, c, s // 4, s % 4, c // 2, c % 2


def remote(src, dst, send_sem, recv_sem, seq, tensor):
    return pltpu.make_async_remote_copy(
        src_ref=src,
        dst_ref=dst,
        send_sem=send_sem,
        recv_sem=recv_sem,
        device_id={"dp": lax.axis_index("dp"), "seq": seq, "tensor": tensor},
        device_id_type=MESH,
    )


def arrived(dst, recv_sem):
    pltpu.make_async_copy(dst, dst, recv_sem).wait()


def greet_signal(partners):
    barrier = pltpu.get_barrier_semaphore()
    for seq, tensor in partners:
        pl.semaphore_signal(
            barrier,
            inc=1,
            device_id={"dp": lax.axis_index("dp"), "seq": seq, "tensor": tensor},
            device_id_type=MESH,
        )


def greet_wait(partners):
    pl.semaphore_wait(pltpu.get_barrier_semaphore(), len(partners))


def greet(partners):
    greet_signal(partners)
    greet_wait(partners)


def normalized(values, gain):
    mean_square = jnp.mean(values * values, axis=-1, keepdims=True)
    gain = gain.reshape((1,) * (values.ndim - 1) + gain.shape)
    return (values * lax.rsqrt(mean_square + EPSILON) * gain).astype(BF16)


class RingSum:
    def __init__(self, send, recv, send_sem, recv_sem, s, z, k):
        self.send, self.recv = send, recv
        self.send_sem, self.recv_sem = send_sem, recv_sem
        self.s, self.z = s, z
        self.up = (z + 1) % 4
        self.down = (z + 3) % 4
        self.far = (z + 2) % 4
        self.up_c = self.up * 2 + k
        self.down_c = self.down * 2 + k

    def copies(self, ch, phase):
        part = pl.ds(0, 2) if phase == 0 else pl.ds(2, 1)
        made = []
        for d, target in ((0, self.up_c), (1, self.down_c)):
            made.append(
                remote(
                    self.send.at[ch, d, part],
                    self.recv.at[ch, d, part],
                    self.send_sem.at[ch, d, phase],
                    self.recv_sem.at[ch, d, phase],
                    self.s,
                    target,
                )
            )
        return made

    def first(self, ch, value):
        self.send[ch, 0, 0] = value(self.far, 0).astype(BF16)
        self.send[ch, 0, 1] = value(self.up, 1).astype(BF16)
        self.send[ch, 1, 0] = value(self.far, 1).astype(BF16)
        self.send[ch, 1, 1] = value(self.down, 0).astype(BF16)
        for copy in self.copies(ch, 0):
            copy.start()

    def second(self, ch, value):
        for copy in self.copies(ch, 0):
            copy.wait_recv()
        self.send[ch, 0, 2] = (value(self.up, 0) + self.recv[ch, 0, 0].astype(F32)).astype(BF16)
        self.send[ch, 1, 2] = (value(self.down, 1) + self.recv[ch, 1, 0].astype(F32)).astype(BF16)
        for copy in self.copies(ch, 1):
            copy.start()

    def third(self, ch, value):
        for copy in self.copies(ch, 1):
            copy.wait_recv()
        one = (
            value(self.z, 0)
            + self.recv[ch, 0, 2].astype(F32)
            + self.recv[ch, 1, 1].astype(F32)
        )
        two = (
            value(self.z, 1)
            + self.recv[ch, 0, 1].astype(F32)
            + self.recv[ch, 1, 2].astype(F32)
        )
        return one, two

    def finish(self, ch):
        for phase in range(2):
            for copy in self.copies(ch, phase):
                copy.wait_send()


def rope_table(groups, base_rows):
    half = HEAD_DIM // 2
    frequency = ROPE_BASE ** (-(np.arange(half, dtype=np.float64) / half))
    angles = np.arange(groups * base_rows, dtype=np.float64)[:, None] * frequency[None, :]
    cosine, sine = np.cos(angles), np.sin(angles)
    table = np.concatenate([cosine, cosine, -sine, sine], axis=1).astype(np.float32)
    return table.reshape(groups, 16, 2, 2, 16, 4 * half)


ORDER = (
    "G0", "H0", "W1", "D0", "W2", "H1", "A0", "D1", "H2", "A1", "D2", "W3",
    "H3", "B0", "A2", "D3", "B1", "C0", "A3", "B2", "C1", "N0", "B3", "C2",
    "N1", "C3", "R0", "N2", "R1", "N3", "Q0", "W4", "R2", "Q1", "F0", "Q2",
    "R3", "F1", "Q3", "E0", "F2", "E1", "F3", "E2", "W5", "E3",
)


GATHERS = 15


def front_kernel(
    tok_hbm, mlp_gain_ref, wg_hbm, wu_hbm, wd_hbm, attn_gain_ref, q_hbm, k_hbm, v_hbm, o_hbm, table_hbm,
    stream_ref, q_out, kv_out, wo_out,
    tok, wg, wu, wd, xn, hid, mine, csend, crecv, zsend, zrecv, sstage, xg, w, tab, qst, kvst,
    tok_sem, gu_sem, wd_sem, wsem_s, wsem_r, csem_s, csem_r, zsem_s, zsem_r, ssem_s, ssem_r,
    w_sem, tab_sem, own_s, own_r, relay_s, relay_r, q_s, q_r, kv_s, kv_r, yf_s, yf_r,
    f1_s, f1_r, f2_s, f2_r, g_s, g_r,
):
    s, c, y, x, z, k = place()
    sib = c + 1 - 2 * k
    ff = wg.shape[1]
    width = tok.shape[1]
    gu_tiles = 4
    gu_cols = ff // gu_tiles
    up, down, far = (z + 1) % 4, (z + 3) % 4, (z + 2) % 4
    up_c, down_c = up * 2 + k, down * 2 + k
    other_s = (1 - y) * 4 + x
    core_of_rows = x // 2

    def pair_of(ch):
        return (s // 2 + 1 + ch) % 4

    def source_of(ch, pair):
        return (pair + 3 - ch) % 4

    def tok_copies(ch):
        a = pair_of(ch) * 2
        low = pl.ds(pl.multiple_of(a * 64, 128), 128)
        high = pl.ds(pl.multiple_of((14 - a) * 64, 128), 128)
        return [
            pltpu.make_async_copy(tok_hbm.at[low], tok.at[low], tok_sem.at[ch, 0]),
            pltpu.make_async_copy(tok_hbm.at[high], tok.at[high], tok_sem.at[ch, 1]),
        ]

    def gu_copies(n):
        cols = pl.ds(n * gu_cols, gu_cols)
        return [
            pltpu.make_async_copy(wg_hbm.at[:, cols], wg.at[:, cols], gu_sem.at[n, 0]),
            pltpu.make_async_copy(wu_hbm.at[:, cols], wu.at[:, cols], gu_sem.at[n, 1]),
        ]

    wd_copy = pltpu.make_async_copy(wd_hbm, wd, wd_sem.at[0])
    own_weights = [
        pltpu.make_async_copy(src, w.at[i], w_sem.at[i]) for i, src in enumerate((q_hbm, k_hbm, v_hbm))
    ]
    table_copies = [
        pltpu.make_async_copy(
            table_hbm.at[:, 15 - s if half else s, :, k], tab.at[:, half], tab_sem.at[half]
        )
        for half in range(2)
    ]
    weight_sends = [
        remote(src, dst, wsem_s.at[i], wsem_r.at[i], s, sib)
        for i, (src, dst) in enumerate(
            ((q_hbm, w.at[3]), (k_hbm, w.at[4]), (v_hbm, w.at[5]))
        )
    ]

    partners = [(s, sib), (s, up_c), (s, down_c)]
    partners += [((s + d) % 8, c) for d in range(1, 8)]
    partners += [(y * 4 + (x + d) % 4, sib) for d in range(1, 4)]
    for copy in tok_copies(0):
        copy.start()
    for n in range(gu_tiles):
        for copy in gu_copies(n):
            copy.start()
    greet_signal(partners)
    wd_copy.start()
    for ch in range(1, 4):
        for copy in tok_copies(ch):
            copy.start()
    for copy in own_weights + table_copies:
        copy.start()

    def token_rows(ch):
        a = pair_of(ch) * 2
        low = tok[pl.ds(pl.multiple_of(a * 64, 128), 128), :]
        high = tok[pl.ds(pl.multiple_of((14 - a) * 64, 128), 128), :]
        return low, high

    def step_H(ch):
        for copy in tok_copies(ch):
            copy.wait()
        low, high = token_rows(ch)
        gain = mlp_gain_ref[...].astype(F32)
        xn[0:128, :] = normalized(low.astype(F32), gain)
        xn[128:256, :] = normalized(high.astype(F32), gain)
        for n in range(gu_tiles):
            if ch == 0:
                for copy in gu_copies(n):
                    copy.wait()
            cols = slice(n * gu_cols, (n + 1) * gu_cols)
            gate = jnp.dot(xn[...], wg[:, cols], preferred_element_type=F32)
            up_part = jnp.dot(xn[...], wu[:, cols], preferred_element_type=F32)
            hid[:, cols] = (gate / (1.0 + jnp.exp(-gate)) * up_part).astype(BF16)

    def core_copy(ch):
        return remote(csend.at[ch], crecv.at[ch], csem_s.at[ch], csem_r.at[ch], s, sib)

    def step_G(ch):
        greet_wait(partners)
        for copy in weight_sends:
            copy.start()
        gather_own().start()
        for d in range(2):
            gather(d).start()

    def step_D(ch):
        if ch == 0:
            wd_copy.wait()
        cols_n = 256
        for n in range(width // cols_n):
            cols = slice(n * cols_n, (n + 1) * cols_n)
            part = jnp.dot(hid[...], wd[:, cols], preferred_element_type=F32)
            part = part.reshape(4, 2, 2, 16, cols_n)
            even, odd = part[:, :, 0], part[:, :, 1]
            mine[ch, :, :, :, cols] = jnp.where(k == 0, even, odd)
            csend[ch, :, :, :, cols] = jnp.where(k == 0, odd, even).astype(BF16)
        core_copy(ch).start()

    x_up, x_down, x_far = (x + 1) % 4, (x + 3) % 4, (x + 2) % 4
    slice_rows = o_hbm.shape[0] // 8

    def gather_own():
        mine_rows = o_hbm.at[pl.ds(pl.multiple_of(slice_rows * s, slice_rows), slice_rows)]
        return pltpu.make_async_copy(mine_rows, wo_out.at[z, k, y, x], g_r.at[GATHERS])

    def gather(i):
        half = slice_rows // 2
        if i < 2:
            src = o_hbm.at[pl.ds(pl.multiple_of(slice_rows * s, slice_rows), slice_rows)]
            dst, to = wo_out.at[z, k, y, x], (s, up_c if i == 0 else down_c)
        elif i < 4:
            d = i - 2
            dst = wo_out.at[up if d else down, k, y, x, pl.ds(d * half, half)]
            src, to = dst, (s, down_c if d else up_c)
        elif i == 4:
            dst = wo_out.at[:, k, y, x]
            src, to = dst, (other_s, c)
        elif i < 9:
            d = (i - 5) % 2
            dst = wo_out.at[:, k, y if i < 7 else 1 - y, x]
            src, to = dst, (y * 4 + (x_down if d else x_up), c)
        elif i < 11:
            d = i - 9
            dst = wo_out.at[pl.ds(2 * d, 2), k, :, x_up if d else x_down]
            src, to = dst, (y * 4 + (x_down if d else x_up), c)
        else:
            dst = wo_out.at[:, k, :, (x, x_up, x_down, x_far)[i - 11]]
            src, to = dst, (s, sib)
        return remote(src, dst, g_s.at[i], g_r.at[i], *to)

    def gather_wait(i):
        half = slice_rows // 2
        if i < 2:
            dst = wo_out.at[up if i else down, k, y, x]
        elif i < 4:
            dst = wo_out.at[far, k, y, x, pl.ds((i - 2) * half, half)]
        elif i == 4:
            dst = wo_out.at[:, k, 1 - y, x]
        elif i < 9:
            dst = wo_out.at[:, k, y if i < 7 else 1 - y, x_up if (i - 5) % 2 else x_down]
        elif i < 11:
            dst = wo_out.at[pl.ds(2 * (i - 9), 2), k, :, x_far]
        else:
            dst = wo_out.at[:, 1 - k, :, (x, x_up, x_down, x_far)[i - 11]]
        arrived(dst, g_r.at[i])

    def step_W(i):
        waits, starts = (
            ((0, 1), (2, 3)),
            ((2, 3), (4, 5, 6)),
            ((4,), (7, 8, 11)),
            ((5, 6, 7, 8), (9, 10, 12, 13)),
            ((9, 10), (14,)),
        )[i - 1]
        if i == 2:
            gather_own().wait()
        for j in waits:
            gather_wait(j)
        for j in starts:
            gather(j).start()

    ring = RingSum(zsend, zrecv, zsem_s, zsem_r, s, z, k)

    def piece(ch):
        def value(zd, t):
            block = jnp.where(zd < 2, t, 3 - t)
            return mine[ch, block, zd % 2] + crecv[ch, block, zd % 2].astype(F32)

        return value

    def step_A(ch):
        core_copy(ch).wait_recv()
        ring.first(ch, piece(ch))

    def step_B(ch):
        ring.second(ch, piece(ch))

    def seq_copy(ch, t, target):
        return remote(
            sstage.at[ch, t], stream_ref.at[s], ssem_s.at[ch, t], ssem_r.at[s], target, c
        )

    def step_C(ch):
        totals = ring.third(ch, piece(ch))
        a = pair_of(ch) * 2
        for t in range(2):
            block = jnp.where(z < 2, a + t, 15 - a - t)
            start = pl.multiple_of(block * 64 + (2 * (z % 2) + k) * 16, 16)
            rows = tok[pl.ds(start, 16), :].astype(F32)
            result = (totals[t] + rows).astype(BF16)
            if ch < 3:
                sstage[ch, t] = result
                seq_copy(ch, t, a + t).start()
            else:

                @pl.when(s == a + t)
                def _():
                    stream_ref[s] = result

                @pl.when(s != a + t)
                def _():
                    sstage[ch, t] = result
                    seq_copy(ch, t, a + t).start()

    def own_copies(ch):
        return [
            remote(xg.at[ch, :, z], xg.at[ch, :, z], own_s.at[ch, d], own_r.at[ch, d], s, target)
            for d, target in ((0, up_c), (1, down_c))
        ]

    def step_N(ch):
        g = 2 * source_of(ch, s // 2)
        if ch < 3:
            for t in range(2):
                arrived(stream_ref.at[g + t], ssem_r.at[g + t])
        else:
            other = g + 1 - s % 2
            arrived(stream_ref.at[other], ssem_r.at[other])
        gain = attn_gain_ref[...].astype(F32)
        xg[ch, :, z] = normalized(stream_ref[pl.ds(g, 2)].astype(F32), gain)
        for copy in own_copies(ch):
            copy.start()

    def relay_copies(ch):
        return [
            remote(
                xg.at[ch, d, source], xg.at[ch, d, source],
                relay_s.at[ch, d], relay_r.at[ch, d], s, target,
            )
            for d, source, target in ((0, down, up_c), (1, up, down_c))
        ]

    def step_R(ch):
        arrived(xg.at[ch, :, down], own_r.at[ch, 0])
        arrived(xg.at[ch, :, up], own_r.at[ch, 1])
        for copy in relay_copies(ch):
            copy.start()

    def out_rows(ch, sy, sx):
        return pl.ds(4 * source_of(ch, 2 * sy + sx // 2), 4)

    def q_far(ch, d):
        hx = (x + d) % 4
        return remote(
            qst.at[ch, hx], q_out.at[out_rows(ch, y, x), x % 2, :, k],
            q_s.at[ch, d], q_r.at[ch, x % 2, k], y * 4 + hx, z * 2 + core_of_rows,
        )

    def q_near(ch):
        return pltpu.make_async_copy(
            qst.at[ch, x], q_out.at[out_rows(ch, y, x), x % 2, :, k], q_r.at[ch, x % 2, k]
        )

    def kv_send(ch, d):
        hx = (x + d) % 4
        src = kvst.at[ch, hx]
        dst = kv_out.at[out_rows(ch, y, x), s, :, k]
        if d == 0:
            return pltpu.make_async_copy(src, dst, kv_r.at[ch, x])
        return remote(src, dst, kv_s.at[ch, d], kv_r.at[ch, x], y * 4 + hx, c)

    def y_forward(ch, d):
        sx = (x + d) % 4
        part = kv_out.at[out_rows(ch, y, sx), y * 4 + sx, :, k]
        src = kvst.at[ch, x] if d == 0 else part
        return remote(src, part, yf_s.at[ch, d], yf_r.at[ch, sx], other_s, c)

    def core_forwards(ch, which):
        sy = y if which == 0 else 1 - y
        send, recv = (f1_s, f1_r) if which == 0 else (f2_s, f2_r)
        made = []
        for h in range(2):
            part = kv_out.at[out_rows(ch, sy, 2 * h), pl.ds(sy * 4 + 2 * h, 2), :, k]
            made.append(remote(part, part, send.at[ch, h], recv.at[ch, h], s, sib))
        return made

    def rope(values, cosine, sine):
        return values * cosine + pltpu.roll(values, HEAD_DIM // 2, 1) * sine

    def step_Q(ch):
        for d in range(2):
            arrived(xg.at[ch, d, far], relay_r.at[ch, d])
        if ch == 0:
            for copy in own_weights + table_copies:
                copy.wait()
            for i, copy in enumerate(weight_sends):
                copy.wait_recv()
        lhs = xg[ch].reshape(128, width)
        trig = tab[pl.ds(2 * source_of(ch, s // 2), 2)].reshape(128, 2 * HEAD_DIM)
        cosine, sine = trig[:, :HEAD_DIM], trig[:, HEAD_DIM:]
        for part in range(2):
            core = k if part == 0 else 1 - k
            kf = jnp.dot(lhs, w[3 * part + 1], preferred_element_type=F32)
            vf = jnp.dot(lhs, w[3 * part + 2], preferred_element_type=F32)
            qf = jnp.dot(lhs, w[3 * part], preferred_element_type=F32)
            for hh in range(2):
                cols = slice(hh * HEAD_DIM, (hh + 1) * HEAD_DIM)
                hx = 2 * core + hh
                qst[ch, hx] = rope(qf[:, cols], cosine, sine).astype(BF16).reshape(4, 2, 16, HEAD_DIM)
                kvst[ch, hx, :, :, :, :HEAD_DIM] = (
                    rope(kf[:, cols], cosine, sine).astype(BF16).reshape(4, 2, 16, HEAD_DIM)
                )
                kvst[ch, hx, :, :, :, HEAD_DIM:] = vf[:, cols].astype(BF16).reshape(4, 2, 16, HEAD_DIM)
        for d in (2, 1, 3, 0):
            kv_send(ch, d).start()
        y_forward(ch, 0).start()
        for d in (2, 1, 3):
            q_far(ch, d).start()

        @pl.when(core_of_rows == k)
        def _():
            q_near(ch).start()

        @pl.when(core_of_rows != k)
        def _():
            q_far(ch, 0).start()

    def step_F(ch):
        for d in (1, 3, 2, 0):
            sx = (x + d) % 4
            arrived(kv_out.at[out_rows(ch, y, sx), y * 4 + sx, :, k], kv_r.at[ch, sx])
            if d:
                y_forward(ch, d).start()
        for copy in core_forwards(ch, 0):
            copy.start()

    def step_E(ch):
        for sx in range(4):
            arrived(kv_out.at[out_rows(ch, 1 - y, sx), (1 - y) * 4 + sx, :, k], yf_r.at[ch, sx])
        for copy in core_forwards(ch, 1):
            copy.start()

    steps = dict(
        H=step_H, G=step_G, D=step_D, A=step_A, B=step_B, C=step_C, N=step_N, R=step_R, Q=step_Q,
        F=step_F, E=step_E, W=step_W,
    )
    for name in ORDER:
        steps[name[0]](int(name[1]))

    for ch in range(4):
        core_copy(ch).wait_send()
        ring.finish(ch)
        a = pair_of(ch) * 2
        for t in range(2):
            if ch < 3:
                seq_copy(ch, t, a + t).wait_send()
            else:

                @pl.when(s != a + t)
                def _():
                    seq_copy(ch, t, a + t).wait_send()

        for copy in own_copies(ch) + relay_copies(ch):
            copy.wait_send()
        for d in range(4):
            if d:
                kv_send(ch, d).wait_send()
                q_far(ch, d).wait_send()
            y_forward(ch, d).wait_send()

        @pl.when(core_of_rows != k)
        def _():
            q_far(ch, 0).wait_send()

        for which in range(2):
            for copy in core_forwards(ch, which):
                copy.wait_send()
        for aa in range(2):
            sx = 2 * k + aa
            for kk in range(2):
                arrived(q_out.at[out_rows(ch, y, sx), aa, :, kk], q_r.at[ch, aa, kk])
        for h in range(2):
            for sy, recv in ((y, f1_r), (1 - y, f2_r)):
                arrived(
                    kv_out.at[out_rows(ch, sy, 2 * h), pl.ds(sy * 4 + 2 * h, 2), :, 1 - k],
                    recv.at[ch, h],
                )
    for copy in weight_sends:
        copy.wait_send()
    for i in range(GATHERS):
        gather(i).wait_send()
    for i in range(11, GATHERS):
        gather_wait(i)


def attention_kernel(doc_ref, q_ref, kv_ref, out_ref, *, chunks, tile):
    log2e = 1.4426950408889634
    factor = HEAD_DIM ** (-0.5) * log2e
    s, c, y, x, z, k = place()
    first_block = 4 * y + 2 * k
    starts_of = [jnp.sum((doc_ref[...] < d).astype(jnp.int32)) for d in range(1, 4)]

    def row_start(position):
        start = jnp.zeros_like(position)
        for d in range(3):
            start = jnp.where(starts_of[d] <= position, starts_of[d], start)
        return start

    def low_first(g):
        return g * (2 * tile) + first_block * 64

    def high_first(g):
        return g * (2 * tile) + (14 - first_block) * 64

    def low_positions(g):
        row = lax.broadcasted_iota(jnp.int32, (128, 1), 0)
        return low_first(g) + row

    def high_positions(g):
        row = lax.broadcasted_iota(jnp.int32, (128, 1), 0)
        return high_first(g) + jnp.where(row < 64, row + 64, row - 64)

    def key_positions(t):
        col = lax.broadcasted_iota(jnp.int32, (1, tile), 1)
        flipped = (tile // 64 - 1 - col // 64) * 64 + col % 64
        return t * tile + jnp.where(t % 2 == 0, col, flipped)

    def scored(queries, t, allowed):
        scores = lax.dot_general(
            queries, kv_ref[t, :, :HEAD_DIM], (((1,), (1,)), ((), ())), preferred_element_type=F32
        ) * factor
        return scores if allowed is None else jnp.where(allowed, scores, NEGATIVE)

    def top(scores):
        return jnp.max(scores, axis=1, keepdims=True)

    def lanes(weights):
        return sum(weights[:, i * 128 : (i + 1) * 128] for i in range(tile // 128))

    def mixed(weights, t):
        return jnp.dot(weights.astype(BF16), kv_ref[t, :, HEAD_DIM:], preferred_element_type=F32)

    def update(state, queries, tiles, allowed):
        highest, total, weighted = state
        scores = [scored(queries, t, allowed and allowed[i]) for i, t in enumerate(tiles)]
        new_highest = highest
        for part in scores:
            new_highest = jnp.maximum(new_highest, top(part))
        rescale = jnp.exp2(highest - new_highest)
        total, weighted = total * rescale, weighted * rescale
        for part, t in zip(scores, tiles):
            weights = jnp.exp2(part - new_highest)
            total = total + lanes(weights)
            weighted = weighted + mixed(weights, t)
        return new_highest, total, weighted

    def one_chunk(g, carry):
        queries = q_ref[pl.ds(2 * g, 2)].reshape(256, HEAD_DIM)
        positions = jnp.concatenate([low_positions(g), high_positions(g)], axis=0)
        starts = row_start(positions)
        first_tile = row_start(low_first(g)) // tile
        last_start = row_start(high_first(g) + 127)
        plain_tile = jnp.clip((last_start + tile - 1) // tile, first_tile, 2 * g)
        plain_tile = plain_tile + plain_tile % 2

        t = 2 * g
        where_keys = key_positions(t)
        near = scored(queries, t, (where_keys <= positions) & (where_keys >= starts))
        where_keys = key_positions(t + 1)
        allowed = (where_keys <= positions[128:]) & (where_keys >= starts[128:])
        last = scored(queries[128:], t + 1, allowed)
        highest = top(near)
        high = jnp.maximum(highest[128:], top(last))
        highest = jnp.concatenate([highest[:128], high], axis=0)
        near = jnp.exp2(near - highest)
        last = jnp.exp2(last - high)
        total, weighted = lanes(near), mixed(near, t)
        total = jnp.concatenate([total[:128], total[128:] + lanes(last)], axis=0)
        weighted = jnp.concatenate([weighted[:128], weighted[128:] + mixed(last, t + 1)], axis=0)
        state = highest, total, weighted

        def masked_step(t, state):
            pair = (2 * t, 2 * t + 1)
            return update(state, queries, pair, [key_positions(i) >= starts for i in pair])

        def plain_step(i, state):
            return update(state, queries, (2 * i, 2 * i + 1), None)

        state = lax.fori_loop(first_tile // 2, plain_tile // 2, masked_step, state)
        highest, total, weighted = lax.fori_loop(plain_tile // 2, g, plain_step, state)
        result = weighted / jnp.sum(total, axis=1, keepdims=True)
        out_ref[pl.ds(2 * g, 2)] = result.astype(BF16).reshape(2, 128, HEAD_DIM)
        return carry

    lax.fori_loop(0, chunks, one_chunk, 0, unroll=2)


def out_kernel(ctx_ref, stream_ref, wo_hbm, out_ref, cbuf, w, w_sem, x_s, x_r):
    s, c, y, x, z, k = place()
    width = w.shape[1]
    weight_copy = pltpu.make_async_copy(wo_hbm, w, w_sem.at[0])
    weight_copy.start()
    here = x // 2 == k
    barrier = pltpu.get_barrier_semaphore()
    for sx in range(4):
        for sz in range(4):
            seq, tensor = y * 4 + sx, sz * 2 + x // 2

            @pl.when(jnp.logical_not((seq == s) & (tensor == c)))
            def _():
                pl.semaphore_signal(
                    barrier,
                    inc=1,
                    device_id={"dp": lax.axis_index("dp"), "seq": seq, "tensor": tensor},
                    device_id_type=MESH,
                )

    @pl.when(here)
    def _():
        pl.semaphore_wait(barrier, 15)

    @pl.when(jnp.logical_not(here))
    def _():
        pl.semaphore_wait(barrier, 16)

    head = 4 * z + x

    def send(dx, dz, dk):
        aa, tz, tk = (x + dx) % 2, (z + dz) % 4, (k + dk) % 2
        src = ctx_ref.at[:, tz // 2, aa, tz % 2, tk]
        target = y * 4 + 2 * k + aa, tz * 2 + tk
        return src, target

    def far_send(dx, dz, dk):
        src, target = send(dx, dz, dk)
        return remote(src, cbuf.at[head], x_s.at[dx, dz, dk], x_r.at[head], *target)

    def near_send():
        src, _ = send(0, 0, 0)
        return pltpu.make_async_copy(src, cbuf.at[head], x_r.at[head])

    others = [(dx, dz, dk) for dz in (2, 1, 3, 0) for dx in range(2) for dk in range(2)]
    for where in others:
        if where != (0, 0, 0):
            far_send(*where).start()

    @pl.when(here)
    def _():
        near_send().start()

    @pl.when(jnp.logical_not(here))
    def _():
        far_send(0, 0, 0).start()

    weight_copy.wait()
    for h in range(16):
        arrived(cbuf.at[h], x_r.at[h])
    lhs = jnp.concatenate([cbuf[h].reshape(128, HEAD_DIM) for h in range(16)], axis=1)
    cols_n = 256
    for n in range(width // cols_n):
        cols = slice(n * cols_n, (n + 1) * cols_n)
        part = jnp.dot(lhs, w[:, cols], preferred_element_type=F32)
        rows = stream_ref[:, :, cols].astype(F32)
        out_ref[:, :, cols] = (part.reshape(rows.shape) + rows).astype(BF16)

    for where in others:
        if where != (0, 0, 0):
            far_send(*where).wait_send()

    @pl.when(jnp.logical_not(here))
    def _():
        far_send(0, 0, 0).wait_send()


ANY = pl.BlockSpec(memory_space=pl.ANY)
VM = pl.BlockSpec(memory_space=pltpu.VMEM)
SM = pl.BlockSpec(memory_space=pltpu.SMEM)
DMA = pltpu.SemaphoreType.DMA


def params(collective_id):
    return pltpu.CompilerParams(
        collective_id=collective_id, has_side_effects=True, vmem_limit_bytes=VMEM_LIMIT
    )


def like(array):
    return jax.ShapeDtypeStruct(array.shape, array.dtype)


def front(tokens, mlp_gain, gate, up, down, attn_gain, query, key, value, out, table):
    rows, width = tokens.shape
    ff = gate.shape[1]
    cols = query.shape[1]
    return pl.pallas_call(
        front_kernel,
        name="front",
        out_shape=[
            jax.ShapeDtypeStruct((8, 16, width), BF16),
            jax.ShapeDtypeStruct((16, 2, 2, 2, 16, HEAD_DIM), BF16),
            jax.ShapeDtypeStruct((16, 8, 2, 2, 16, 2 * HEAD_DIM), BF16),
            jax.ShapeDtypeStruct((4, 2, 2, 4, out.shape[0] // 8, width), BF16),
        ],
        in_specs=[ANY, VM, ANY, ANY, ANY, VM] + [ANY] * 5,
        out_specs=[VM, ANY, ANY, ANY],
        scratch_shapes=[
            pltpu.VMEM((rows, width), BF16),
            pltpu.VMEM((width, ff), BF16),
            pltpu.VMEM((width, ff), BF16),
            pltpu.VMEM((ff, width), BF16),
            pltpu.VMEM((256, width), BF16),
            pltpu.VMEM((256, ff), BF16),
            pltpu.VMEM((4, 4, 2, 16, width), F32),
            pltpu.VMEM((4, 4, 2, 16, width), BF16),
            pltpu.VMEM((4, 4, 2, 16, width), BF16),
            pltpu.VMEM((4, 2, 3, 16, width), BF16),
            pltpu.VMEM((4, 2, 3, 16, width), BF16),
            pltpu.VMEM((4, 2, 16, width), BF16),
            pltpu.VMEM((4, 2, 4, 16, width), BF16),
            pltpu.VMEM((6, width, cols), BF16),
            pltpu.VMEM((8, 2, 2, 16, 2 * HEAD_DIM), F32),
            pltpu.VMEM((4, 4, 4, 2, 16, HEAD_DIM), BF16),
            pltpu.VMEM((4, 4, 4, 2, 16, 2 * HEAD_DIM), BF16),
            DMA((4, 2)), DMA((4, 2)), DMA((1,)), DMA((3,)), DMA((3,)), DMA((4,)), DMA((4,)),
            DMA((4, 2, 2)), DMA((4, 2, 2)), DMA((4, 2)), DMA((8,)),
            DMA((3,)), DMA((2,)),
            DMA((4, 2)), DMA((4, 2)), DMA((4, 2)), DMA((4, 2)),
            DMA((4, 4)), DMA((4, 2, 2)), DMA((4, 4)), DMA((4, 4)),
            DMA((4, 4)), DMA((4, 4)), DMA((4, 2)), DMA((4, 2)), DMA((4, 2)), DMA((4, 2)),
            DMA((GATHERS,)), DMA((GATHERS + 1,)),
        ],
        compiler_params=params(1),
    )(tokens, mlp_gain, gate, up, down, attn_gain, query, key, value, out, table)


def attend(docs, queries, keys_values):
    tiles = keys_values.shape[0]
    tile = keys_values.shape[1]
    return pl.pallas_call(
        functools.partial(attention_kernel, chunks=tiles // 2, tile=tile),
        name="attend",
        out_shape=like(queries),
        in_specs=[VM, VM, VM],
        out_specs=VM,
        compiler_params=pltpu.CompilerParams(vmem_limit_bytes=VMEM_LIMIT),
    )(docs.reshape(-1, 128), queries, keys_values)


def merge(context, stream, out_weight):
    width = stream.shape[-1]
    return pl.pallas_call(
        out_kernel,
        name="merge",
        out_shape=like(stream),
        in_specs=[ANY, VM, ANY],
        out_specs=VM,
        scratch_shapes=[
            pltpu.VMEM((16, 8, 16, HEAD_DIM), BF16),
            pltpu.VMEM(out_weight.shape, BF16),
            DMA((1,)), DMA((2, 4, 2)), DMA((16,)),
        ],
        compiler_params=params(3),
    )(context, stream, out_weight)


def body(
    tokens, doc_ids, mlp_gain, gate_weight, up_weight, down_weight,
    attn_gain, query_weight, key_weight, value_weight, out_weight,
):
    table = jnp.asarray(rope_table(8, tokens.shape[0]))
    stream, queries, keys_values, whole_out = front(
        tokens, mlp_gain, gate_weight, up_weight, down_weight, attn_gain,
        query_weight, key_weight, value_weight, out_weight, table,
    )
    context = attend(
        doc_ids, queries.reshape(16, 128, HEAD_DIM), keys_values.reshape(16, 512, 2 * HEAD_DIM)
    )
    merged = merge(
        context.reshape(8, 2, 2, 2, 2, 16, HEAD_DIM), stream, whole_out.reshape(-1, tokens.shape[1])
    )
    return merged.reshape(128, tokens.shape[1])


def solution(mesh):
    in_specs = (
        P(("dp", "seq"), None),
        P("dp"),
        P(),
        P(None, "tensor"),
        P(None, "tensor"),
        P("tensor", None),
        P(),
        P(None, "tensor"),
        P(None, "tensor"),
        P(None, "tensor"),
        P("tensor", None),
    )
    out_specs = P(("dp", "seq", "tensor"), None)
    return jax.shard_map(body, mesh=mesh, in_specs=in_specs, out_specs=out_specs, check_vma=False)
```

```python
import functools

import jax
import jax.numpy as jnp
import numpy as np
from jax import lax
from jax.experimental import pallas as pl
from jax.experimental.pallas import tpu as pltpu
from jax.sharding import PartitionSpec as P

HEAD_DIM = 128
EPSILON = 1e-05
ROPE_BASE = 500000.0
NEGATIVE = -1e30
MESH = pl.DeviceIdType.MESH
F32 = jnp.float32
BF16 = jnp.bfloat16
VMEM_LIMIT = 60 * 1024 * 1024


def place():
    s = lax.axis_index("seq")
    c = lax.axis_index("tensor")
    return s, c, s // 4, s % 4, c // 2, c % 2


def remote(src, dst, send_sem, recv_sem, seq, tensor):
    return pltpu.make_async_remote_copy(
        src_ref=src,
        dst_ref=dst,
        send_sem=send_sem,
        recv_sem=recv_sem,
        device_id={"dp": lax.axis_index("dp"), "seq": seq, "tensor": tensor},
        device_id_type=MESH,
    )


def arrived(dst, recv_sem):
    pltpu.make_async_copy(dst, dst, recv_sem).wait()


def greet_signal(partners):
    barrier = pltpu.get_barrier_semaphore()
    for seq, tensor in partners:
        pl.semaphore_signal(
            barrier,
            inc=1,
            device_id={"dp": lax.axis_index("dp"), "seq": seq, "tensor": tensor},
            device_id_type=MESH,
        )


def greet_wait(partners):
    pl.semaphore_wait(pltpu.get_barrier_semaphore(), len(partners))


def greet(partners):
    greet_signal(partners)
    greet_wait(partners)


def normalized(values, gain):
    mean_square = jnp.mean(values * values, axis=-1, keepdims=True)
    gain = gain.reshape((1,) * (values.ndim - 1) + gain.shape)
    return (values * lax.rsqrt(mean_square + EPSILON) * gain).astype(BF16)


class RingSum:
    def __init__(self, send, recv, send_sem, recv_sem, s, z, k):
        self.send, self.recv = send, recv
        self.send_sem, self.recv_sem = send_sem, recv_sem
        self.s, self.z = s, z
        self.up = (z + 1) % 4
        self.down = (z + 3) % 4
        self.far = (z + 2) % 4
        self.up_c = self.up * 2 + k
        self.down_c = self.down * 2 + k

    def copies(self, ch, phase):
        part = pl.ds(0, 2) if phase == 0 else pl.ds(2, 1)
        made = []
        for d, target in ((0, self.up_c), (1, self.down_c)):
            made.append(
                remote(
                    self.send.at[ch, d, part],
                    self.recv.at[ch, d, part],
                    self.send_sem.at[ch, d, phase],
                    self.recv_sem.at[ch, d, phase],
                    self.s,
                    target,
                )
            )
        return made

    def first(self, ch, value):
        self.send[ch, 0, 0] = value(self.far, 0).astype(BF16)
        self.send[ch, 0, 1] = value(self.up, 1).astype(BF16)
        self.send[ch, 1, 0] = value(self.far, 1).astype(BF16)
        self.send[ch, 1, 1] = value(self.down, 0).astype(BF16)
        for copy in self.copies(ch, 0):
            copy.start()

    def second(self, ch, value):
        for copy in self.copies(ch, 0):
            copy.wait_recv()
        self.send[ch, 0, 2] = (value(self.up, 0) + self.recv[ch, 0, 0].astype(F32)).astype(BF16)
        self.send[ch, 1, 2] = (value(self.down, 1) + self.recv[ch, 1, 0].astype(F32)).astype(BF16)
        for copy in self.copies(ch, 1):
            copy.start()

    def third(self, ch, value):
        for copy in self.copies(ch, 1):
            copy.wait_recv()
        one = (
            value(self.z, 0)
            + self.recv[ch, 0, 2].astype(F32)
            + self.recv[ch, 1, 1].astype(F32)
        )
        two = (
            value(self.z, 1)
            + self.recv[ch, 0, 1].astype(F32)
            + self.recv[ch, 1, 2].astype(F32)
        )
        return one, two

    def finish(self, ch):
        for phase in range(2):
            for copy in self.copies(ch, phase):
                copy.wait_send()


def rope_table(groups, base_rows):
    half = HEAD_DIM // 2
    frequency = ROPE_BASE ** (-(np.arange(half, dtype=np.float64) / half))
    angles = np.arange(groups * base_rows, dtype=np.float64)[:, None] * frequency[None, :]
    cosine, sine = np.cos(angles), np.sin(angles)
    table = np.concatenate([cosine, cosine, -sine, sine], axis=1).astype(np.float32)
    return table.reshape(groups, 16, 2, 2, 16, 4 * half)


ORDER = (
    "G0", "H0", "W1", "D0", "W2", "H1", "A0", "D1", "H2", "A1", "D2", "W3",
    "H3", "B0", "A2", "D3", "B1", "C0", "A3", "B2", "C1", "N0", "B3", "C2",
    "N1", "C3", "R0", "N2", "R1", "N3", "Q0", "W4", "R2", "Q1", "F0", "Q2",
    "R3", "F1", "Q3", "E0", "F2", "E1", "F3", "E2", "W5", "E3",
)


GATHERS = 15


def front_kernel(
    tok_hbm, mlp_gain_ref, wg_hbm, wu_hbm, wd_hbm, attn_gain_ref, q_hbm, k_hbm, v_hbm, o_hbm, table_hbm,
    stream_ref, q_out, kv_out, wo_out,
    tok, wg, wu, wd, xn, hid, mine, csend, crecv, zsend, zrecv, sstage, xg, w, tab, qst, kvst,
    tok_sem, gu_sem, wd_sem, wsem_s, wsem_r, csem_s, csem_r, zsem_s, zsem_r, ssem_s, ssem_r,
    w_sem, tab_sem, own_s, own_r, relay_s, relay_r, q_s, q_r, kv_s, kv_r, yf_s, yf_r,
    f1_s, f1_r, f2_s, f2_r, g_s, g_r,
):
    s, c, y, x, z, k = place()
    sib = c + 1 - 2 * k
    ff = wg.shape[1]
    width = tok.shape[1]
    gu_tiles = 4
    gu_cols = ff // gu_tiles
    up, down, far = (z + 1) % 4, (z + 3) % 4, (z + 2) % 4
    up_c, down_c = up * 2 + k, down * 2 + k
    other_s = (1 - y) * 4 + x
    core_of_rows = x // 2

    def pair_of(ch):
        return (s // 2 + 1 + ch) % 4

    def source_of(ch, pair):
        return (pair + 3 - ch) % 4

    def tok_copies(ch):
        a = pair_of(ch) * 2
        low = pl.ds(pl.multiple_of(a * 64, 128), 128)
        high = pl.ds(pl.multiple_of((14 - a) * 64, 128), 128)
        return [
            pltpu.make_async_copy(tok_hbm.at[low], tok.at[low], tok_sem.at[ch, 0]),
            pltpu.make_async_copy(tok_hbm.at[high], tok.at[high], tok_sem.at[ch, 1]),
        ]

    def gu_copies(n):
        cols = pl.ds(n * gu_cols, gu_cols)
        return [
            pltpu.make_async_copy(wg_hbm.at[:, cols], wg.at[:, cols], gu_sem.at[n, 0]),
            pltpu.make_async_copy(wu_hbm.at[:, cols], wu.at[:, cols], gu_sem.at[n, 1]),
        ]

    wd_copy = pltpu.make_async_copy(wd_hbm, wd, wd_sem.at[0])
    own_weights = [
        pltpu.make_async_copy(src, w.at[i], w_sem.at[i]) for i, src in enumerate((q_hbm, k_hbm, v_hbm))
    ]
    table_copies = [
        pltpu.make_async_copy(
            table_hbm.at[:, 15 - s if half else s, :, k], tab.at[:, half], tab_sem.at[half]
        )
        for half in range(2)
    ]
    weight_sends = [
        remote(src, dst, wsem_s.at[i], wsem_r.at[i], s, sib)
        for i, (src, dst) in enumerate(
            ((q_hbm, w.at[3]), (k_hbm, w.at[4]), (v_hbm, w.at[5]))
        )
    ]

    partners = [(s, sib), (s, up_c), (s, down_c)]
    partners += [((s + d) % 8, c) for d in range(1, 8)]
    partners += [(y * 4 + (x + d) % 4, sib) for d in range(1, 4)]
    for copy in tok_copies(0):
        copy.start()
    for n in range(gu_tiles):
        for copy in gu_copies(n):
            copy.start()
    greet_signal(partners)

    def late_loads():
        wd_copy.start()
        for ch in range(1, 4):
            for copy in tok_copies(ch):
                copy.start()
        for copy in own_weights + table_copies:
            copy.start()

    def token_rows(ch):
        a = pair_of(ch) * 2
        low = tok[pl.ds(pl.multiple_of(a * 64, 128), 128), :]
        high = tok[pl.ds(pl.multiple_of((14 - a) * 64, 128), 128), :]
        return low, high

    def step_H(ch):
        for copy in tok_copies(ch):
            copy.wait()
        low, high = token_rows(ch)
        gain = mlp_gain_ref[...].astype(F32)
        xn[0:128, :] = normalized(low.astype(F32), gain)
        xn[128:256, :] = normalized(high.astype(F32), gain)
        for n in range(gu_tiles):
            if ch == 0:
                for copy in gu_copies(n):
                    copy.wait()
                if n == 1:
                    late_loads()
            cols = slice(n * gu_cols, (n + 1) * gu_cols)
            gate = jnp.dot(xn[...], wg[:, cols], preferred_element_type=F32)
            up_part = jnp.dot(xn[...], wu[:, cols], preferred_element_type=F32)
            hid[:, cols] = (gate / (1.0 + jnp.exp(-gate)) * up_part).astype(BF16)

    def core_copy(ch):
        return remote(csend.at[ch], crecv.at[ch], csem_s.at[ch], csem_r.at[ch], s, sib)

    def step_G(ch):
        greet_wait(partners)
        for copy in weight_sends:
            copy.start()
        gather_own().start()
        for d in range(2):
            gather(d).start()

    def step_D(ch):
        if ch == 0:
            wd_copy.wait()
        cols_n = 256
        for n in range(width // cols_n):
            cols = slice(n * cols_n, (n + 1) * cols_n)
            part = jnp.dot(hid[...], wd[:, cols], preferred_element_type=F32)
            part = part.reshape(4, 2, 2, 16, cols_n)
            even, odd = part[:, :, 0], part[:, :, 1]
            mine[ch, :, :, :, cols] = jnp.where(k == 0, even, odd)
            csend[ch, :, :, :, cols] = jnp.where(k == 0, odd, even).astype(BF16)
        core_copy(ch).start()

    x_up, x_down, x_far = (x + 1) % 4, (x + 3) % 4, (x + 2) % 4
    slice_rows = o_hbm.shape[0] // 8

    def gather_own():
        mine_rows = o_hbm.at[pl.ds(pl.multiple_of(slice_rows * s, slice_rows), slice_rows)]
        return pltpu.make_async_copy(mine_rows, wo_out.at[z, k, y, x], g_r.at[GATHERS])

    def gather(i):
        half = slice_rows // 2
        if i < 2:
            src = o_hbm.at[pl.ds(pl.multiple_of(slice_rows * s, slice_rows), slice_rows)]
            dst, to = wo_out.at[z, k, y, x], (s, up_c if i == 0 else down_c)
        elif i < 4:
            d = i - 2
            dst = wo_out.at[up if d else down, k, y, x, pl.ds(d * half, half)]
            src, to = dst, (s, down_c if d else up_c)
        elif i == 4:
            dst = wo_out.at[:, k, y, x]
            src, to = dst, (other_s, c)
        elif i < 9:
            d = (i - 5) % 2
            dst = wo_out.at[:, k, y if i < 7 else 1 - y, x]
            src, to = dst, (y * 4 + (x_down if d else x_up), c)
        elif i < 11:
            d = i - 9
            dst = wo_out.at[pl.ds(2 * d, 2), k, :, x_up if d else x_down]
            src, to = dst, (y * 4 + (x_down if d else x_up), c)
        else:
            dst = wo_out.at[:, k, :, (x, x_up, x_down, x_far)[i - 11]]
            src, to = dst, (s, sib)
        return remote(src, dst, g_s.at[i], g_r.at[i], *to)

    def gather_wait(i):
        half = slice_rows // 2
        if i < 2:
            dst = wo_out.at[up if i else down, k, y, x]
        elif i < 4:
            dst = wo_out.at[far, k, y, x, pl.ds((i - 2) * half, half)]
        elif i == 4:
            dst = wo_out.at[:, k, 1 - y, x]
        elif i < 9:
            dst = wo_out.at[:, k, y if i < 7 else 1 - y, x_up if (i - 5) % 2 else x_down]
        elif i < 11:
            dst = wo_out.at[pl.ds(2 * (i - 9), 2), k, :, x_far]
        else:
            dst = wo_out.at[:, 1 - k, :, (x, x_up, x_down, x_far)[i - 11]]
        arrived(dst, g_r.at[i])

    def step_W(i):
        waits, starts = (
            ((0, 1), (2, 3)),
            ((2, 3), (4, 5, 6)),
            ((4,), (7, 8, 11)),
            ((5, 6, 7, 8), (9, 10, 12, 13)),
            ((9, 10), (14,)),
        )[i - 1]
        if i == 2:
            gather_own().wait()
        for j in waits:
            gather_wait(j)
        for j in starts:
            gather(j).start()

    ring = RingSum(zsend, zrecv, zsem_s, zsem_r, s, z, k)

    def piece(ch):
        def value(zd, t):
            block = jnp.where(zd < 2, t, 3 - t)
            return mine[ch, block, zd % 2] + crecv[ch, block, zd % 2].astype(F32)

        return value

    def step_A(ch):
        core_copy(ch).wait_recv()
        ring.first(ch, piece(ch))

    def step_B(ch):
        ring.second(ch, piece(ch))

    def seq_copy(ch, t, target):
        return remote(
            sstage.at[ch, t], stream_ref.at[s], ssem_s.at[ch, t], ssem_r.at[s], target, c
        )

    def step_C(ch):
        totals = ring.third(ch, piece(ch))
        a = pair_of(ch) * 2
        for t in range(2):
            block = jnp.where(z < 2, a + t, 15 - a - t)
            start = pl.multiple_of(block * 64 + (2 * (z % 2) + k) * 16, 16)
            rows = tok[pl.ds(start, 16), :].astype(F32)
            result = (totals[t] + rows).astype(BF16)
            if ch < 3:
                sstage[ch, t] = result
                seq_copy(ch, t, a + t).start()
            else:

                @pl.when(s == a + t)
                def _():
                    stream_ref[s] = result

                @pl.when(s != a + t)
                def _():
                    sstage[ch, t] = result
                    seq_copy(ch, t, a + t).start()

    def own_copies(ch):
        return [
            remote(xg.at[ch, :, z], xg.at[ch, :, z], own_s.at[ch, d], own_r.at[ch, d], s, target)
            for d, target in ((0, up_c), (1, down_c))
        ]

    def step_N(ch):
        g = 2 * source_of(ch, s // 2)
        if ch < 3:
            for t in range(2):
                arrived(stream_ref.at[g + t], ssem_r.at[g + t])
        else:
            other = g + 1 - s % 2
            arrived(stream_ref.at[other], ssem_r.at[other])
        gain = attn_gain_ref[...].astype(F32)
        xg[ch, :, z] = normalized(stream_ref[pl.ds(g, 2)].astype(F32), gain)
        for copy in own_copies(ch):
            copy.start()

    def relay_copies(ch):
        return [
            remote(
                xg.at[ch, d, source], xg.at[ch, d, source],
                relay_s.at[ch, d], relay_r.at[ch, d], s, target,
            )
            for d, source, target in ((0, down, up_c), (1, up, down_c))
        ]

    def step_R(ch):
        arrived(xg.at[ch, :, down], own_r.at[ch, 0])
        arrived(xg.at[ch, :, up], own_r.at[ch, 1])
        for copy in relay_copies(ch):
            copy.start()

    def out_rows(ch, sy, sx):
        return pl.ds(4 * source_of(ch, 2 * sy + sx // 2), 4)

    def q_far(ch, d):
        hx = (x + d) % 4
        return remote(
            qst.at[ch, hx], q_out.at[out_rows(ch, y, x), x % 2, :, k],
            q_s.at[ch, d], q_r.at[ch, x % 2, k], y * 4 + hx, z * 2 + core_of_rows,
        )

    def q_near(ch):
        return pltpu.make_async_copy(
            qst.at[ch, x], q_out.at[out_rows(ch, y, x), x % 2, :, k], q_r.at[ch, x % 2, k]
        )

    def kv_send(ch, d):
        hx = (x + d) % 4
        src = kvst.at[ch, hx]
        dst = kv_out.at[out_rows(ch, y, x), s, :, k]
        if d == 0:
            return pltpu.make_async_copy(src, dst, kv_r.at[ch, x])
        return remote(src, dst, kv_s.at[ch, d], kv_r.at[ch, x], y * 4 + hx, c)

    def y_forward(ch, d):
        sx = (x + d) % 4
        part = kv_out.at[out_rows(ch, y, sx), y * 4 + sx, :, k]
        src = kvst.at[ch, x] if d == 0 else part
        return remote(src, part, yf_s.at[ch, d], yf_r.at[ch, sx], other_s, c)

    def core_forwards(ch, which):
        sy = y if which == 0 else 1 - y
        send, recv = (f1_s, f1_r) if which == 0 else (f2_s, f2_r)
        made = []
        for h in range(2):
            part = kv_out.at[out_rows(ch, sy, 2 * h), pl.ds(sy * 4 + 2 * h, 2), :, k]
            made.append(remote(part, part, send.at[ch, h], recv.at[ch, h], s, sib))
        return made

    def rope(values, cosine, sine):
        return values * cosine + pltpu.roll(values, HEAD_DIM // 2, 1) * sine

    def step_Q(ch):
        for d in range(2):
            arrived(xg.at[ch, d, far], relay_r.at[ch, d])
        if ch == 0:
            for copy in own_weights + table_copies:
                copy.wait()
            for i, copy in enumerate(weight_sends):
                copy.wait_recv()
        lhs = xg[ch].reshape(128, width)
        trig = tab[pl.ds(2 * source_of(ch, s // 2), 2)].reshape(128, 2 * HEAD_DIM)
        cosine, sine = trig[:, :HEAD_DIM], trig[:, HEAD_DIM:]
        for part in range(2):
            core = k if part == 0 else 1 - k
            kf = jnp.dot(lhs, w[3 * part + 1], preferred_element_type=F32)
            vf = jnp.dot(lhs, w[3 * part + 2], preferred_element_type=F32)
            qf = jnp.dot(lhs, w[3 * part], preferred_element_type=F32)
            for hh in range(2):
                cols = slice(hh * HEAD_DIM, (hh + 1) * HEAD_DIM)
                hx = 2 * core + hh
                qst[ch, hx] = rope(qf[:, cols], cosine, sine).astype(BF16).reshape(4, 2, 16, HEAD_DIM)
                kvst[ch, hx, :, :, :, :HEAD_DIM] = (
                    rope(kf[:, cols], cosine, sine).astype(BF16).reshape(4, 2, 16, HEAD_DIM)
                )
                kvst[ch, hx, :, :, :, HEAD_DIM:] = vf[:, cols].astype(BF16).reshape(4, 2, 16, HEAD_DIM)
        for d in (2, 1, 3, 0):
            kv_send(ch, d).start()
        y_forward(ch, 0).start()
        for d in (2, 1, 3):
            q_far(ch, d).start()

        @pl.when(core_of_rows == k)
        def _():
            q_near(ch).start()

        @pl.when(core_of_rows != k)
        def _():
            q_far(ch, 0).start()

    def step_F(ch):
        for d in (1, 3, 2, 0):
            sx = (x + d) % 4
            arrived(kv_out.at[out_rows(ch, y, sx), y * 4 + sx, :, k], kv_r.at[ch, sx])
            if d:
                y_forward(ch, d).start()
        for copy in core_forwards(ch, 0):
            copy.start()

    def step_E(ch):
        for sx in range(4):
            arrived(kv_out.at[out_rows(ch, 1 - y, sx), (1 - y) * 4 + sx, :, k], yf_r.at[ch, sx])
        for copy in core_forwards(ch, 1):
            copy.start()

    steps = dict(
        H=step_H, G=step_G, D=step_D, A=step_A, B=step_B, C=step_C, N=step_N, R=step_R, Q=step_Q,
        F=step_F, E=step_E, W=step_W,
    )
    for name in ORDER:
        steps[name[0]](int(name[1]))

    for ch in range(4):
        core_copy(ch).wait_send()
        ring.finish(ch)
        a = pair_of(ch) * 2
        for t in range(2):
            if ch < 3:
                seq_copy(ch, t, a + t).wait_send()
            else:

                @pl.when(s != a + t)
                def _():
                    seq_copy(ch, t, a + t).wait_send()

        for copy in own_copies(ch) + relay_copies(ch):
            copy.wait_send()
        for d in range(4):
            if d:
                kv_send(ch, d).wait_send()
                q_far(ch, d).wait_send()
            y_forward(ch, d).wait_send()

        @pl.when(core_of_rows != k)
        def _():
            q_far(ch, 0).wait_send()

        for which in range(2):
            for copy in core_forwards(ch, which):
                copy.wait_send()
        for aa in range(2):
            sx = 2 * k + aa
            for kk in range(2):
                arrived(q_out.at[out_rows(ch, y, sx), aa, :, kk], q_r.at[ch, aa, kk])
        for h in range(2):
            for sy, recv in ((y, f1_r), (1 - y, f2_r)):
                arrived(
                    kv_out.at[out_rows(ch, sy, 2 * h), pl.ds(sy * 4 + 2 * h, 2), :, 1 - k],
                    recv.at[ch, h],
                )
    for copy in weight_sends:
        copy.wait_send()
    for i in range(GATHERS):
        gather(i).wait_send()
    for i in range(11, GATHERS):
        gather_wait(i)


def attention_kernel(doc_ref, q_ref, kv_ref, out_ref, *, chunks, tile):
    log2e = 1.4426950408889634
    factor = HEAD_DIM ** (-0.5) * log2e
    s, c, y, x, z, k = place()
    first_block = 4 * y + 2 * k
    starts_of = [jnp.sum((doc_ref[...] < d).astype(jnp.int32)) for d in range(1, 4)]

    def row_start(position):
        start = jnp.zeros_like(position)
        for d in range(3):
            start = jnp.where(starts_of[d] <= position, starts_of[d], start)
        return start

    def low_first(g):
        return g * (2 * tile) + first_block * 64

    def high_first(g):
        return g * (2 * tile) + (14 - first_block) * 64

    def low_positions(g):
        row = lax.broadcasted_iota(jnp.int32, (128, 1), 0)
        return low_first(g) + row

    def high_positions(g):
        row = lax.broadcasted_iota(jnp.int32, (128, 1), 0)
        return high_first(g) + jnp.where(row < 64, row + 64, row - 64)

    def key_positions(t):
        col = lax.broadcasted_iota(jnp.int32, (1, tile), 1)
        flipped = (tile // 64 - 1 - col // 64) * 64 + col % 64
        return t * tile + jnp.where(t % 2 == 0, col, flipped)

    def scored(queries, t, allowed):
        scores = lax.dot_general(
            queries, kv_ref[t, :, :HEAD_DIM], (((1,), (1,)), ((), ())), preferred_element_type=F32
        ) * factor
        return scores if allowed is None else jnp.where(allowed, scores, NEGATIVE)

    def top(scores):
        return jnp.max(scores, axis=1, keepdims=True)

    def lanes(weights):
        return sum(weights[:, i * 128 : (i + 1) * 128] for i in range(tile // 128))

    def mixed(weights, t):
        return jnp.dot(weights.astype(BF16), kv_ref[t, :, HEAD_DIM:], preferred_element_type=F32)

    def update(state, queries, tiles, allowed):
        highest, total, weighted = state
        scores = [scored(queries, t, allowed and allowed[i]) for i, t in enumerate(tiles)]
        new_highest = highest
        for part in scores:
            new_highest = jnp.maximum(new_highest, top(part))
        rescale = jnp.exp2(highest - new_highest)
        total, weighted = total * rescale, weighted * rescale
        for part, t in zip(scores, tiles):
            weights = jnp.exp2(part - new_highest)
            total = total + lanes(weights)
            weighted = weighted + mixed(weights, t)
        return new_highest, total, weighted

    def one_chunk(g, carry):
        queries = q_ref[pl.ds(2 * g, 2)].reshape(256, HEAD_DIM)
        positions = jnp.concatenate([low_positions(g), high_positions(g)], axis=0)
        starts = row_start(positions)
        first_tile = row_start(low_first(g)) // tile
        last_start = row_start(high_first(g) + 127)
        plain_tile = jnp.clip((last_start + tile - 1) // tile, first_tile, 2 * g)
        plain_tile = plain_tile + plain_tile % 2

        t = 2 * g
        where_keys = key_positions(t)
        near = scored(queries, t, (where_keys <= positions) & (where_keys >= starts))
        where_keys = key_positions(t + 1)
        allowed = (where_keys <= positions[128:]) & (where_keys >= starts[128:])
        last = scored(queries[128:], t + 1, allowed)
        highest = top(near)
        high = jnp.maximum(highest[128:], top(last))
        highest = jnp.concatenate([highest[:128], high], axis=0)
        near = jnp.exp2(near - highest)
        last = jnp.exp2(last - high)
        total, weighted = lanes(near), mixed(near, t)
        total = jnp.concatenate([total[:128], total[128:] + lanes(last)], axis=0)
        weighted = jnp.concatenate([weighted[:128], weighted[128:] + mixed(last, t + 1)], axis=0)
        state = highest, total, weighted

        def masked_step(t, state):
            pair = (2 * t, 2 * t + 1)
            return update(state, queries, pair, [key_positions(i) >= starts for i in pair])

        def plain_step(i, state):
            return update(state, queries, (2 * i, 2 * i + 1), None)

        state = lax.fori_loop(first_tile // 2, plain_tile // 2, masked_step, state)
        highest, total, weighted = lax.fori_loop(plain_tile // 2, g, plain_step, state)
        result = weighted / jnp.sum(total, axis=1, keepdims=True)
        out_ref[pl.ds(2 * g, 2)] = result.astype(BF16).reshape(2, 128, HEAD_DIM)
        return carry

    lax.fori_loop(0, chunks, one_chunk, 0, unroll=2)


def out_kernel(ctx_ref, stream_ref, wo_hbm, out_ref, cbuf, w, w_sem, x_s, x_r):
    s, c, y, x, z, k = place()
    width = w.shape[1]
    weight_copy = pltpu.make_async_copy(wo_hbm, w, w_sem.at[0])
    weight_copy.start()
    here = x // 2 == k
    barrier = pltpu.get_barrier_semaphore()
    for sx in range(4):
        for sz in range(4):
            seq, tensor = y * 4 + sx, sz * 2 + x // 2

            @pl.when(jnp.logical_not((seq == s) & (tensor == c)))
            def _():
                pl.semaphore_signal(
                    barrier,
                    inc=1,
                    device_id={"dp": lax.axis_index("dp"), "seq": seq, "tensor": tensor},
                    device_id_type=MESH,
                )

    @pl.when(here)
    def _():
        pl.semaphore_wait(barrier, 15)

    @pl.when(jnp.logical_not(here))
    def _():
        pl.semaphore_wait(barrier, 16)

    head = 4 * z + x

    def send(dx, dz, dk):
        aa, tz, tk = (x + dx) % 2, (z + dz) % 4, (k + dk) % 2
        src = ctx_ref.at[:, tz // 2, aa, tz % 2, tk]
        target = y * 4 + 2 * k + aa, tz * 2 + tk
        return src, target

    def far_send(dx, dz, dk):
        src, target = send(dx, dz, dk)
        return remote(src, cbuf.at[head], x_s.at[dx, dz, dk], x_r.at[head], *target)

    def near_send():
        src, _ = send(0, 0, 0)
        return pltpu.make_async_copy(src, cbuf.at[head], x_r.at[head])

    others = [(dx, dz, dk) for dz in (2, 1, 3, 0) for dx in range(2) for dk in range(2)]
    for where in others:
        if where != (0, 0, 0):
            far_send(*where).start()

    @pl.when(here)
    def _():
        near_send().start()

    @pl.when(jnp.logical_not(here))
    def _():
        far_send(0, 0, 0).start()

    weight_copy.wait()
    for h in range(16):
        arrived(cbuf.at[h], x_r.at[h])
    lhs = jnp.concatenate([cbuf[h].reshape(128, HEAD_DIM) for h in range(16)], axis=1)
    cols_n = 256
    for n in range(width // cols_n):
        cols = slice(n * cols_n, (n + 1) * cols_n)
        part = jnp.dot(lhs, w[:, cols], preferred_element_type=F32)
        rows = stream_ref[:, :, cols].astype(F32)
        out_ref[:, :, cols] = (part.reshape(rows.shape) + rows).astype(BF16)

    for where in others:
        if where != (0, 0, 0):
            far_send(*where).wait_send()

    @pl.when(jnp.logical_not(here))
    def _():
        far_send(0, 0, 0).wait_send()


ANY = pl.BlockSpec(memory_space=pl.ANY)
VM = pl.BlockSpec(memory_space=pltpu.VMEM)
SM = pl.BlockSpec(memory_space=pltpu.SMEM)
DMA = pltpu.SemaphoreType.DMA


def params(collective_id):
    return pltpu.CompilerParams(
        collective_id=collective_id, has_side_effects=True, vmem_limit_bytes=VMEM_LIMIT
    )


def like(array):
    return jax.ShapeDtypeStruct(array.shape, array.dtype)


def front(tokens, mlp_gain, gate, up, down, attn_gain, query, key, value, out, table):
    rows, width = tokens.shape
    ff = gate.shape[1]
    cols = query.shape[1]
    return pl.pallas_call(
        front_kernel,
        name="front",
        out_shape=[
            jax.ShapeDtypeStruct((8, 16, width), BF16),
            jax.ShapeDtypeStruct((16, 2, 2, 2, 16, HEAD_DIM), BF16),
            jax.ShapeDtypeStruct((16, 8, 2, 2, 16, 2 * HEAD_DIM), BF16),
            jax.ShapeDtypeStruct((4, 2, 2, 4, out.shape[0] // 8, width), BF16),
        ],
        in_specs=[ANY, VM, ANY, ANY, ANY, VM] + [ANY] * 5,
        out_specs=[VM, ANY, ANY, ANY],
        scratch_shapes=[
            pltpu.VMEM((rows, width), BF16),
            pltpu.VMEM((width, ff), BF16),
            pltpu.VMEM((width, ff), BF16),
            pltpu.VMEM((ff, width), BF16),
            pltpu.VMEM((256, width), BF16),
            pltpu.VMEM((256, ff), BF16),
            pltpu.VMEM((4, 4, 2, 16, width), F32),
            pltpu.VMEM((4, 4, 2, 16, width), BF16),
            pltpu.VMEM((4, 4, 2, 16, width), BF16),
            pltpu.VMEM((4, 2, 3, 16, width), BF16),
            pltpu.VMEM((4, 2, 3, 16, width), BF16),
            pltpu.VMEM((4, 2, 16, width), BF16),
            pltpu.VMEM((4, 2, 4, 16, width), BF16),
            pltpu.VMEM((6, width, cols), BF16),
            pltpu.VMEM((8, 2, 2, 16, 2 * HEAD_DIM), F32),
            pltpu.VMEM((4, 4, 4, 2, 16, HEAD_DIM), BF16),
            pltpu.VMEM((4, 4, 4, 2, 16, 2 * HEAD_DIM), BF16),
            DMA((4, 2)), DMA((4, 2)), DMA((1,)), DMA((3,)), DMA((3,)), DMA((4,)), DMA((4,)),
            DMA((4, 2, 2)), DMA((4, 2, 2)), DMA((4, 2)), DMA((8,)),
            DMA((3,)), DMA((2,)),
            DMA((4, 2)), DMA((4, 2)), DMA((4, 2)), DMA((4, 2)),
            DMA((4, 4)), DMA((4, 2, 2)), DMA((4, 4)), DMA((4, 4)),
            DMA((4, 4)), DMA((4, 4)), DMA((4, 2)), DMA((4, 2)), DMA((4, 2)), DMA((4, 2)),
            DMA((GATHERS,)), DMA((GATHERS + 1,)),
        ],
        compiler_params=params(1),
    )(tokens, mlp_gain, gate, up, down, attn_gain, query, key, value, out, table)


def attend(docs, queries, keys_values):
    tiles = keys_values.shape[0]
    tile = keys_values.shape[1]
    return pl.pallas_call(
        functools.partial(attention_kernel, chunks=tiles // 2, tile=tile),
        name="attend",
        out_shape=like(queries),
        in_specs=[VM, VM, VM],
        out_specs=VM,
        compiler_params=pltpu.CompilerParams(vmem_limit_bytes=VMEM_LIMIT),
    )(docs.reshape(-1, 128), queries, keys_values)


def merge(context, stream, out_weight):
    width = stream.shape[-1]
    return pl.pallas_call(
        out_kernel,
        name="merge",
        out_shape=like(stream),
        in_specs=[ANY, VM, ANY],
        out_specs=VM,
        scratch_shapes=[
            pltpu.VMEM((16, 8, 16, HEAD_DIM), BF16),
            pltpu.VMEM(out_weight.shape, BF16),
            DMA((1,)), DMA((2, 4, 2)), DMA((16,)),
        ],
        compiler_params=params(3),
    )(context, stream, out_weight)


def body(
    tokens, doc_ids, mlp_gain, gate_weight, up_weight, down_weight,
    attn_gain, query_weight, key_weight, value_weight, out_weight,
):
    table = jnp.asarray(rope_table(8, tokens.shape[0]))
    stream, queries, keys_values, whole_out = front(
        tokens, mlp_gain, gate_weight, up_weight, down_weight, attn_gain,
        query_weight, key_weight, value_weight, out_weight, table,
    )
    context = attend(
        doc_ids, queries.reshape(16, 128, HEAD_DIM), keys_values.reshape(16, 512, 2 * HEAD_DIM)
    )
    merged = merge(
        context.reshape(8, 2, 2, 2, 2, 16, HEAD_DIM), stream, whole_out.reshape(-1, tokens.shape[1])
    )
    return merged.reshape(128, tokens.shape[1])


def solution(mesh):
    in_specs = (
        P(("dp", "seq"), None),
        P("dp"),
        P(),
        P(None, "tensor"),
        P(None, "tensor"),
        P("tensor", None),
        P(),
        P(None, "tensor"),
        P(None, "tensor"),
        P(None, "tensor"),
        P("tensor", None),
    )
    out_specs = P(("dp", "seq", "tensor"), None)
    return jax.shard_map(body, mesh=mesh, in_specs=in_specs, out_specs=out_specs, check_vma=False)
```
